768 devices in a mesh: dp: 24 (over x, z_lo, core), fsdp: 32 (over y, z_hi).
Axes of the slice: x: 4, y: 8, z: 12 (z_hi: 4, z_lo: 3; z = z_hi * 3 + z_lo), core: 2. Of those that a mesh axis runs over, the one named last changes fastest.
Arguments:
- student_feat: bfloat16 [18432, 384], P('dp', 'fsdp'), may hold values from -0.3984375 to 0.3984375
- teacher_feat: bfloat16 [4608, 384], P('dp', 'fsdp'), may hold values from -0.3984375 to 0.3984375
- student_proto: bfloat16 [384, 65536], P(None, 'fsdp'), may hold values from -5 to 5
- teacher_proto: float32 [384, 65536], P('dp', 'fsdp'), may hold values from -5 to 5
- center: float32 [65536], P('fsdp'), may hold values from -0.1 to 0.1
Outputs:
- new_teacher: float32 [384, 65536], P('dp', 'fsdp')
- grad_student_feat: float32 [18432, 384], P('dp')
- grad_student_proto: float32 [384, 65536], P('dp', 'fsdp')
The draws below stay inside these ranges and needn't reach their ends.
All inputs are finite; a program needn't handle non-finite values.
Results may differ from the reference program's by a relative error of at most 0.005.
The reference program's roundings to bfloat16 on the way (of `student_rows`, `teacher_rows`, `proto_half`, `teacher_half` and `logit_grads`) count: a program that leaves them out, or rounds other values in their place, can miss the bound.
Values may be sent and summed in bfloat16 or wider, within the bound.
A program may use at most 32 MiB of HBM per device.

```python
import math
import jax
import jax.numpy as jnp
from jax import lax

BOT = 384
PROTO = 65536
STUDENT_CROPS = 8
GLOBAL_CROPS = 2
IMG_DP = 96
S_ROWS = 18432
T_ROWS = 4608


def draw_student_proto(key, part):
    key = jax.random.fold_in(key, 11)
    entry_key, column_key = jax.random.split(key)
    entries = jnp.clip(jax.random.normal(entry_key, (BOT, PROTO), jnp.float32), -5.0, 5.0)
    column = jnp.exp(jax.random.uniform(column_key, (1, PROTO), jnp.float32, math.log(0.1), 0.0))
    return (entries * column).astype(jnp.bfloat16)


def draw_teacher_proto(key, part):
    key = jax.random.fold_in(key, 23)
    entry_key, column_key = jax.random.split(key)
    entries = jnp.clip(jax.random.normal(entry_key, (BOT, PROTO), jnp.float32), -5.0, 5.0)
    column = jnp.exp(jax.random.uniform(column_key, (1, PROTO), jnp.float32, math.log(0.1), 0.0))
    return (entries * column).astype(jnp.float32)


def spiked(array, stream_key, source, target, blocks, factor):
    def block_of(dim):
        return (jnp.arange(array.shape[dim]) // (array.shape[dim] // blocks)).reshape((-1,) + (1,) * (array.ndim - 1 - dim))

    near = jax.random.permutation(stream_key, blocks)[block_of(target)]
    other_side = (block_of(target) + blocks // 2) % blocks
    return jnp.where((block_of(source) == near) | (block_of(source) == other_side), factor * array, array)


def block_levels(own_key, dims, cuts, least, top_value):
    def one(dim, parts):
        heights = jax.random.uniform(jax.random.fold_in(jax.random.fold_in(own_key, 6), dim), (parts,), jnp.float32, least / len(cuts), top_value / len(cuts))
        return jnp.repeat(jnp.exp(heights), dims[dim] // parts).reshape((-1,) + (1,) * (len(dims) - dim - 1))

    loudness = one(*cuts[0])
    for cut in cuts[1:]:
        loudness = loudness * one(*cut)
    return loudness


def normal_values(key, extent, scale, reach, cuts=(), dtype=jnp.bfloat16):
    drawn = scale * jax.random.normal(key, extent, jnp.float32)
    if cuts:
        drawn = drawn * block_levels(key, extent, cuts, -0.22, 0.18)
    return jnp.clip(drawn, -reach, reach).astype(dtype)


def gaussian_with(key, dims, spread, limit, shards, heavy, held_as=jnp.bfloat16):
    result = spread * jax.random.normal(key, dims, jnp.float32)
    if shards:
        result = result * block_levels(key, dims, shards, -0.22, 0.18)
    return jnp.clip(spiked(result, jax.random.fold_in(key, 3), *heavy), -limit, limit).astype(held_as)


def setup_inputs(seed: int = 0) -> dict:
    arg_keys = jax.random.split(jax.random.key(seed), 6)
    student_feat = gaussian_with(arg_keys[0], (S_ROWS, BOT), 0.05, 0.3984375, ((0, 24), (1, 32)), (0, 1, 32, 2.75))
    teacher_feat = normal_values(arg_keys[1], (T_ROWS, BOT), 0.05, 0.3984375, ((0, 24), (1, 32)))
    student_proto = draw_student_proto(jax.random.fold_in(arg_keys[5], 71), 0)
    teacher_proto = draw_teacher_proto(jax.random.fold_in(arg_keys[5], 71), 0)
    center = jnp.clip(jax.random.uniform(arg_keys[4], (PROTO,), jnp.float32, -0.1, 0.1) * block_levels(arg_keys[4], (PROTO,), ((0, 32),), -0.4, 0.0), -0.1, 0.1)
    return dict(student_feat=student_feat, teacher_feat=teacher_feat, student_proto=student_proto, teacher_proto=teacher_proto, center=center)


epsilon = 1e-06
momentum = 0.994
teacher_temp = 0.04
student_temp = 0.1

def unit_rows(values):
    inverse = lax.rsqrt(lax.optimization_barrier(jnp.sum(values * values, axis=1, keepdims=True)) + epsilon)
    return (values * inverse, inverse)

def unit_columns(values):
    inverse = lax.rsqrt(lax.optimization_barrier(jnp.sum(values * values, axis=0, keepdims=True)) + epsilon)
    return (values * inverse, inverse)

def crop_grads(teacher_prob, student_prob):
    images = teacher_prob.shape[0] // GLOBAL_CROPS
    proto_count = teacher_prob.shape[1]
    teacher_view = teacher_prob.reshape(images, GLOBAL_CROPS, proto_count)
    student_view = student_prob.reshape(images, STUDENT_CROPS, proto_count)
    pair_sum = lax.optimization_barrier(jnp.sum(teacher_view, axis=1, keepdims=True))
    partner = jnp.concatenate([pair_sum - teacher_view, jnp.broadcast_to(pair_sum, (images, STUDENT_CROPS - GLOBAL_CROPS, proto_count))], axis=1)
    position = lax.broadcasted_iota(jnp.int32, (1, STUDENT_CROPS, 1), 1)
    counts = jnp.where(position < GLOBAL_CROPS, jnp.float32(GLOBAL_CROPS - 1), jnp.float32(GLOBAL_CROPS))
    loss_scale = jnp.float32(PROTO / 16.0)
    logit_grads = loss_scale * (counts * student_view - partner) / student_temp
    return logit_grads.reshape(images * STUDENT_CROPS, proto_count).astype(jnp.bfloat16)

def reference(student_feat, teacher_feat, student_proto, teacher_proto, center):
    student_unit, student_inv = unit_rows(student_feat.astype(jnp.float32))
    student_rows = student_unit.astype(jnp.bfloat16)
    teacher_unit, teacher_inv = unit_rows(teacher_feat.astype(jnp.float32))
    teacher_rows = teacher_unit.astype(jnp.bfloat16)
    proto_unit, proto_inv = unit_columns(student_proto.astype(jnp.float32))
    proto_half = proto_unit.astype(jnp.bfloat16)
    new_teacher = momentum * teacher_proto + (1.0 - momentum) * student_proto.astype(jnp.float32)
    teacher_unit_cols, teacher_col_inv = unit_columns(new_teacher)
    teacher_half = teacher_unit_cols.astype(jnp.bfloat16)
    blocks = teacher_feat.shape[0] // (GLOBAL_CROPS * IMG_DP)
    student_blocks = student_rows.reshape(blocks, IMG_DP * STUDENT_CROPS, BOT)
    teacher_blocks = teacher_rows.reshape(blocks, IMG_DP * GLOBAL_CROPS, BOT)

    def block_step(running, pieces):
        student_piece, teacher_piece = pieces
        teacher_logits = jnp.dot(teacher_piece, teacher_half, preferred_element_type=jnp.float32)
        teacher_exp = jnp.exp((teacher_logits - center[None, :]) / teacher_temp)
        teacher_prob = teacher_exp / lax.optimization_barrier(jnp.sum(teacher_exp, axis=1, keepdims=True))
        student_logits = jnp.dot(student_piece, proto_half, preferred_element_type=jnp.float32)
        student_exp = jnp.exp(student_logits / student_temp)
        student_prob = student_exp / lax.optimization_barrier(jnp.sum(student_exp, axis=1, keepdims=True))
        logit_grads = crop_grads(teacher_prob, student_prob)
        feat_grads = jnp.dot(logit_grads, proto_half.T, preferred_element_type=jnp.float32)
        running = running + jnp.dot(student_piece.T, logit_grads, preferred_element_type=jnp.float32)
        return (running, feat_grads)
    start_sum = jnp.zeros((BOT, PROTO), jnp.float32)
    proto_raw, feat_grads = lax.scan(block_step, start_sum, (student_blocks, teacher_blocks))
    feat_grads = feat_grads.reshape(-1, BOT)
    grad_student_feat = student_inv * (feat_grads - student_unit * lax.optimization_barrier(jnp.sum(student_unit * feat_grads, axis=1, keepdims=True)))
    grad_student_proto = proto_inv * (proto_raw - proto_unit * lax.optimization_barrier(jnp.sum(proto_unit * proto_raw, axis=0, keepdims=True)))
    return (new_teacher, grad_student_feat, grad_student_proto)
```

```python
import functools

import jax
import jax.numpy as jnp
from jax import lax
from jax.experimental import pallas as pl
from jax.experimental.pallas import tpu as pltpu
from jax.sharding import PartitionSpec as P

NX, NZL, NC = 4, 3, 2
NY, NZH = 8, 4
STUDENT_CROPS = 8
GLOBAL_CROPS = 2
PROTO = 65536
EPSILON = 1e-06
MOMENTUM = 0.994
TEACHER_TEMP = 0.04
STUDENT_TEMP = 0.1
LANES = 128
COLS = 256
MESH = pl.DeviceIdType.MESH
F32 = jnp.float32
BF16 = jnp.bfloat16


def up(value, unit):
    return -(-value // unit) * unit


def hops(members, odd):
    long, short = members // 2, (members - 1) // 2
    return (short, long) if odd else (long, short)


def kernel(
    pack_ref, proto_ref, teacher_ref, center_ref, feat_ref, raw_ref,
    norm_near, norm_x, feats, masters, half, half_t, proto_inv, unit, rows, rows_t, row_inv,
    t_rows, s_exp, t_exp, s_sum, t_sum, scale, den_y, den_z, grads, feat_sum,
    wire_y, land_y, chunk, wire_z, land_z, final,
    raw, wire_c, land_c, wire_x, land_x, own_x, wire_l, land_l,
    send_sem, recv_sem,
):
    d, f = lax.axis_index("dp"), lax.axis_index("fsdp")
    c, zl, x = lax.rem(d, NC), lax.rem(d // NC, NZL), d // (NC * NZL)
    y, zh = f // NZH, lax.rem(f, NZH)
    bot, count = proto_ref.shape
    s_rows = unit.shape[0]
    t_count = t_rows.shape[0]
    t_pad = up(t_count, LANES)
    width = pack_ref.shape[1]
    tiles = count // COLS

    def at(x_=x, zl_=zl, c_=c, y_=y, zh_=zh):
        return ((x_ * NZL + zl_) * NC + c_, y_ * NZH + zh_)

    def wrap(value, size):
        return lax.rem(value + size, size)

    used = [0]
    started = []

    def send(src, dst, to):
        i = used[0]
        used[0] += 1
        copy = pltpu.make_async_remote_copy(
            src_ref=src, dst_ref=dst, send_sem=send_sem.at[i], recv_sem=recv_sem.at[i],
            device_id=to, device_id_type=MESH,
        )
        copy.start()
        started.append(copy)
        return copy

    near = [
        at(zl_=wrap(zl + k, NZL), c_=lax.rem(c + e, NC))
        for k in range(NZL)
        for e in range(NC)
        if k or e
    ]
    partners = (
        [at(y_=wrap(y + k, NY)) for k in range(1, NY)]
        + [at(zh_=wrap(zh + k, NZH)) for k in range(1, NZH)]
        + near
        + [at(x_=wrap(x + k, NX)) for k in range(1, NX)]
    )
    barrier = pltpu.get_barrier_semaphore()
    for partner in partners:
        pl.semaphore_signal(barrier, inc=1, device_id=partner, device_id_type=MESH)

    feats[y, zh] = pack_ref[...]
    student_own = proto_ref[pl.ds(pl.multiple_of(d * 16, 16), 16), :].astype(F32)
    own_master = MOMENTUM * teacher_ref[...] + (1.0 - MOMENTUM) * student_own
    squares = jnp.sum(own_master * own_master, axis=0, keepdims=True)
    line = lax.broadcasted_iota(jnp.int32, (8, count // 8), 0)
    folded = jnp.zeros((8, count // 8), F32)
    for i in range(8):
        folded = jnp.where(line == i, squares[:, i * (count // 8) : (i + 1) * (count // 8)], folded)
    norm_near[0] = folded
    pl.semaphore_wait(barrier, len(partners))
    norms = [send(norm_near.at[0], norm_near.at[i + 1], to) for i, to in enumerate(near)]

    def gather(buffer, members, spot, ring_to, ring_at, ring_size, direct, others, extra=None):
        came = {}
        for k in range(1, others):
            came[k] = send(spot(0, 0), spot(0, 0), direct(k))
        if extra is not None:
            extra(spot(0, 0))
        right, left = {}, {}
        most = ring_size // 2
        for h in range(1, most + 2):
            for k in range(others):
                r_hops, l_hops = hops(ring_size, k % 2)
                if h == 1 and k > 0:
                    came[k].wait_recv()
                    if extra is not None:
                        extra(spot(0, k))
                if h > 1 and h - 1 <= r_hops:
                    right[k, h - 1].wait_recv()
                    if extra is not None:
                        extra(spot(-(h - 1), k))
                if h <= r_hops:
                    right[k, h] = send(spot(-(h - 1), k), spot(-(h - 1), k), ring_to(1))
                if h > 1 and h - 1 <= l_hops:
                    left[k, h - 1].wait_recv()
                    if extra is not None:
                        extra(spot(h - 1, k))
                if h <= l_hops:
                    left[k, h] = send(spot(h - 1, k), spot(h - 1, k), ring_to(-1))
                yield

    def feat_spot(dy, k):
        return feats.at[wrap(y + dy, NY), wrap(zh - k, NZH)]

    def master_spot(dx, k):
        return masters.at[(wrap(x + dx, NX) * NZL + wrap(zl - k, NZL)) * NC + c]

    across = []

    def to_sibling(block):
        across.append(send(block, block, at(c_=1 - c)))

    feat_steps = gather(
        feats, None, feat_spot, lambda s: at(y_=wrap(y + s, NY)), None, NY,
        lambda k: at(zh_=wrap(zh + k, NZH)), NZH,
    )
    master_steps = gather(
        masters, None, master_spot, lambda s: at(x_=wrap(x + s, NX)), None, NX,
        lambda k: at(zl_=wrap(zl + k, NZL)), NZL, to_sibling,
    )
    next(feat_steps)
    for copy in norms:
        copy.wait_recv()
    norm_x[0] = jnp.sum(norm_near[...], axis=0)
    norms = [send(norm_x.at[0], norm_x.at[k], at(x_=wrap(x + k, NX))) for k in range(1, NX)]
    for k in range(1, NZH):
        next(feat_steps)
    for copy in norms:
        copy.wait_recv()
    inverse = lax.rsqrt(jnp.sum(norm_x[...], axis=0) + EPSILON)
    inverse = jnp.concatenate([inverse[i : i + 1] for i in range(8)], axis=1)
    masters[d] = (own_master * inverse).astype(BF16)
    next(master_steps)

    @pl.loop(0, tiles)
    def _(n):
        at_n = pl.ds(pl.multiple_of(n * COLS, COLS), COLS)
        block = proto_ref[:, at_n].astype(F32)
        inverse = lax.rsqrt(jnp.sum(block * block, axis=0, keepdims=True) + EPSILON)
        normed = block * inverse
        half[:, at_n] = normed.astype(BF16)
        half_t[at_n, :] = normed.T.astype(BF16)
        proto_inv[:, at_n] = inverse

    def drain(*steps):
        live = list(steps)
        while live:
            for one in list(live):
                if next(one, live) is live:
                    live.remove(one)

    drain(feat_steps, master_steps)
    for copy in across:
        copy.wait_recv()

    slots = feats[...].reshape(NY * NZH * 16, width)
    spots = lax.broadcasted_iota(jnp.int32, (bot, NY * NZH * 16), 1)
    wanted = lax.broadcasted_iota(jnp.int32, (bot, NY * NZH * 16), 0)
    owner = lax.shift_right_logical(wanted * 5462, 16)
    pick_s = (spots == owner * 16 + (wanted - owner * 12)).astype(F32).astype(BF16)
    pick_t = (spots == owner * 16 + 12 + (wanted & 3)).astype(F32).astype(BF16)
    student_t = jnp.dot(pick_s, slots[:, :s_rows], preferred_element_type=F32)
    inverse = lax.rsqrt(jnp.sum(student_t * student_t, axis=0, keepdims=True) + EPSILON)
    rows_t[...] = (student_t * inverse).astype(BF16)
    student = student_t.T
    inverse = lax.rsqrt(jnp.sum(student * student, axis=1, keepdims=True) + EPSILON)
    normed = student * inverse
    unit[...] = normed
    rows[...] = normed.astype(BF16)
    row_inv[...] = jnp.broadcast_to(inverse, row_inv.shape)
    pieces = jnp.dot(pick_t, slots[:, : 3 * t_pad], preferred_element_type=F32)
    place = lax.broadcasted_iota(jnp.int32, (bot, t_pad), 0)
    owner = lax.shift_right_logical(place * 5462, 16)
    quarter = lax.shift_right_logical(place - owner * 12, 2)
    teacher_t = jnp.where(
        quarter == 0,
        pieces[:, :t_pad],
        jnp.where(quarter == 1, pieces[:, t_pad : 2 * t_pad], pieces[:, 2 * t_pad :]),
    )
    teacher = teacher_t.T[:t_count]
    inverse = lax.rsqrt(jnp.sum(teacher * teacher, axis=1, keepdims=True) + EPSILON)
    t_rows[...] = (teacher * inverse).astype(BF16)

    def fold(values):
        return values[:, :LANES] + values[:, LANES:]

    s_sum[...] = jnp.zeros_like(s_sum)
    t_sum[...] = jnp.zeros_like(t_sum)

    @pl.loop(0, tiles)
    def _(n):
        at_n = pl.ds(pl.multiple_of(n * COLS, COLS), COLS)
        block = masters[:, :, at_n].reshape(bot, COLS)
        logits = jnp.dot(t_rows[...], block, preferred_element_type=F32)
        value = jnp.exp((logits - center_ref[:, at_n]) * (1.0 / TEACHER_TEMP))
        t_exp[:, at_n] = value
        t_sum[:t_count, :] += fold(value)

    @pl.loop(0, tiles)
    def _(n):
        at_n = pl.ds(pl.multiple_of(n * COLS, COLS), COLS)
        logits = jnp.dot(rows[...], half[:, at_n], preferred_element_type=F32)
        value = jnp.exp(logits * (1.0 / STUDENT_TEMP))
        s_exp[:, at_n] = value
        s_sum[:s_rows, :] += fold(value)

    s_tiles, t_tiles = s_sum.shape[0] // LANES, t_sum.shape[0] // LANES
    line = lax.broadcasted_iota(jnp.int32, (8, LANES), 0)
    lane = lax.broadcasted_iota(jnp.int32, (8, LANES), 1)
    packed = jnp.zeros((8, LANES), F32)
    for i in range(s_tiles + t_tiles):
        block = (
            s_sum[i * LANES : (i + 1) * LANES, :]
            if i < s_tiles
            else t_sum[(i - s_tiles) * LANES : (i - s_tiles + 1) * LANES, :]
        )
        packed = jnp.where(line == i, jnp.sum(block.T, axis=0, keepdims=True), packed)
    den_y[0] = packed
    met = [send(den_y.at[0], den_y.at[k], at(y_=wrap(y + k, NY))) for k in range(1, NY)]
    for copy in met:
        copy.wait_recv()
    den_z[0] = jnp.sum(den_y[...], axis=0)
    met = [send(den_z.at[0], den_z.at[k], at(zh_=wrap(zh + k, NZH))) for k in range(1, NZH)]
    for copy in met:
        copy.wait_recv()
    total = jnp.sum(den_z[...], axis=0)
    inverse = (PROTO / 16.0 / STUDENT_TEMP) / jnp.where(total > 0.0, total, 1.0)
    crop = lax.broadcasted_iota(jnp.int32, (LANES, LANES), 0) & (STUDENT_CROPS - 1)
    copies = jnp.where(crop < GLOBAL_CROPS, F32(GLOBAL_CROPS - 1), F32(GLOBAL_CROPS))
    for i in range(s_tiles + t_tiles):
        block = jnp.broadcast_to(inverse[i : i + 1, :], (LANES, LANES)).T
        scale[i * LANES : (i + 1) * LANES, :] = block * copies if i < s_tiles else block

    position = lax.broadcasted_iota(jnp.int32, (STUDENT_CROPS, count), 0)
    group = 4

    @pl.loop(0, t_count // (GLOBAL_CROPS * group))
    def _(i):
        at_t = pl.ds(pl.multiple_of(i * 8, 8), 8)
        at_s = pl.ds(pl.multiple_of(i * 32, 32), 32)
        t_scale = scale[pl.ds(pl.multiple_of(s_tiles * LANES + i * 8, 8), 8), :1]
        prob = t_exp[at_t, :] * t_scale
        value = s_exp[at_s, :] * scale[at_s, :1]
        out = []
        for a in range(group):
            first, second = prob[2 * a : 2 * a + 1], prob[2 * a + 1 : 2 * a + 2]
            partner = jnp.where(
                position == 0, second, jnp.where(position == 1, first, first + second)
            )
            out.append(value[8 * a : 8 * a + 8] - partner)
        grads[at_s, :] = jnp.concatenate(out, axis=0).astype(BF16)

    deep = 512 if count % 512 == 0 else COLS
    feat_sum[...] = jnp.zeros_like(feat_sum)

    @pl.loop(0, count // deep)
    def _(n):
        at_n = pl.ds(pl.multiple_of(n * deep, deep), deep)
        feat_sum[...] += jnp.dot(grads[:, at_n], half_t[at_n, :], preferred_element_type=F32)

    part = feat_sum[...]
    along = jnp.sum(unit[...] * part, axis=1, keepdims=True)
    feat_sum[...] = row_inv[:, :1] * (part - unit[...] * along)

    y_rows = s_rows // NY
    r_hops, l_hops = hops(NY, 0)

    def own_y(j):
        return feat_sum[pl.ds(pl.multiple_of(j * y_rows, 8), y_rows), :]

    def reduce_y():
        right, left = {}, {}
        for h in range(1, r_hops + 1):
            value = own_y(wrap(y + (r_hops + 1 - h), NY))
            if h > 1:
                right[h - 1].wait_recv()
                value = value + land_y[0, h - 2].astype(F32)
            wire_y[0, h - 1] = value.astype(BF16)
            right[h] = send(wire_y.at[0, h - 1], land_y.at[0, h - 1], at(y_=wrap(y + 1, NY)))
            if h <= l_hops:
                value = own_y(wrap(y - (l_hops + 1 - h), NY))
                if h > 1:
                    left[h - 1].wait_recv()
                    value = value + land_y[1, h - 2].astype(F32)
                wire_y[1, h - 1] = value.astype(BF16)
                left[h] = send(wire_y.at[1, h - 1], land_y.at[1, h - 1], at(y_=wrap(y - 1, NY)))
            yield
        value = own_y(y)
        if l_hops:
            left[l_hops].wait_recv()
            value = value + land_y[1, l_hops - 1].astype(F32)
        right[r_hops].wait_recv()
        value = value + land_y[0, r_hops - 1].astype(F32)
        chunk[...] = value.reshape(chunk.shape)
        met = []
        for k in range(1, NZH):
            wire_z[k] = chunk[wrap(zh + k, NZH)].astype(BF16)
            met.append(send(wire_z.at[k], land_z.at[k], at(zh_=wrap(zh + k, NZH))))
        yield
        value = chunk[zh]
        for k in range(1, NZH):
            met[k - 1].wait_recv()
            value = value + land_z[k].astype(F32)
        final[y, zh] = value.astype(BF16)
        yield from gather(
            final, None, lambda dy, k: final.at[wrap(y + dy, NY), wrap(zh - k, NZH)],
            lambda s: at(y_=wrap(y + s, NY)), None, NY,
            lambda k: at(zh_=wrap(zh + k, NZH)), NZH,
        )

    tail = reduce_y()
    next(tail)

    @pl.loop(0, tiles)
    def _(n):
        at_n = pl.ds(pl.multiple_of(n * COLS, COLS), COLS)
        part = jnp.dot(rows_t[...], grads[:, at_n], preferred_element_type=F32)
        inverse = proto_inv[:, at_n]
        normed = proto_ref[:, at_n].astype(F32) * inverse
        along = jnp.sum(normed * part, axis=0, keepdims=True)
        part = inverse * (part - normed * along)
        raw[:, :, :, at_n] = part.reshape(NX * NZL, NC, 16, COLS)
        wire_c[:, :, at_n] = raw[:, pl.ds(1 - c, 1), :, at_n].reshape(NX * NZL, 16, COLS).astype(BF16)

    def reduce_x():
        over = {}
        for k in range(NX):
            block = wrap(x + (NX // 2 + 2 * NX - k), 2 * NX)
            block = lax.rem(block, NX)
            at_k = pl.ds(block * NZL, NZL)
            over[NX // 2 - k] = send(wire_c.at[at_k], land_c.at[at_k], at(c_=1 - c))
        for copy in over.values():
            copy.wait_recv()

        def own(dx, k):
            slot = wrap(x + dx, NX) * NZL + k
            return raw[slot, c] + land_c[slot].astype(F32)

        right, left = {}, {}
        for h in range(1, NX // 2 + 1):
            for k in range(NZL):
                r_hops, l_hops = hops(NX, k % 2)
                if h <= r_hops:
                    value = own(r_hops + 1 - h, k)
                    if h > 1:
                        right[k, h - 1].wait_recv()
                        value = value + land_x[0, k, h - 2].astype(F32)
                    wire_x[0, k, h - 1] = value.astype(BF16)
                    right[k, h] = send(
                        wire_x.at[0, k, h - 1], land_x.at[0, k, h - 1], at(x_=wrap(x + 1, NX))
                    )
                if h <= l_hops:
                    value = own(-(l_hops + 1 - h), k)
                    if h > 1:
                        left[k, h - 1].wait_recv()
                        value = value + land_x[1, k, h - 2].astype(F32)
                    wire_x[1, k, h - 1] = value.astype(BF16)
                    left[k, h] = send(
                        wire_x.at[1, k, h - 1], land_x.at[1, k, h - 1], at(x_=wrap(x - 1, NX))
                    )
                yield
        for k in range(NZL):
            r_hops, l_hops = hops(NX, k % 2)
            value = own(0, k)
            if l_hops:
                left[k, l_hops].wait_recv()
                value = value + land_x[1, k, l_hops - 1].astype(F32)
            if r_hops:
                right[k, r_hops].wait_recv()
                value = value + land_x[0, k, r_hops - 1].astype(F32)
            own_x[k] = value
        met = []
        for k in range(1, NZL):
            wire_l[k] = own_x[wrap(zl + k, NZL)].astype(BF16)
            met.append(send(wire_l.at[k], land_l.at[k], at(zl_=wrap(zl + k, NZL))))
        yield
        value = own_x[zl]
        for k in range(1, NZL):
            met[k - 1].wait_recv()
            value = value + land_l[k].astype(F32)
        raw_ref[...] = value

    drain(tail, reduce_x())
    for i in range(NY):
        feat_ref[i * y_rows : (i + 1) * y_rows, :] = (
            final[i].astype(F32).reshape(y_rows, bot).astype(BF16)
        )

    for copy in started:
        copy.wait_send()


def call(pack, proto, teacher, center, s_rows, t_rows):
    bot, count = proto.shape
    y_rows = s_rows // NY
    z_rows = y_rows // NZH
    width = pack.shape[1]
    vmem = pltpu.VMEM
    ring, short = NY // 2, NX // 2
    s_pad, t_pad = up(s_rows, LANES), up(t_rows, LANES)
    copies = (
        (NZL * NC - 1) + (NX - 1) + (NZH - 1) + NZH * (NY - 1)
        + (NZL - 1) + NZL * (NX - 1) + NZL * NX
        + (NY - 1) + (NZH - 1)
        + (NY - 1) + (NZH - 1) + (NZH - 1) + NZH * (NY - 1)
        + NX + NZL * (NX - 1) + (NZL - 1)
    )
    return pl.pallas_call(
        kernel,
        out_shape=(
            jax.ShapeDtypeStruct((s_rows, bot), BF16),
            jax.ShapeDtypeStruct((16, count), F32),
        ),
        in_specs=[pl.BlockSpec(memory_space=pltpu.VMEM)] * 4,
        out_specs=[pl.BlockSpec(memory_space=pltpu.VMEM)] * 2,
        scratch_shapes=[
            vmem((NZL * NC, 8, count // 8), F32),
            vmem((NX, 8, count // 8), F32),
            vmem((NY, NZH, 16, width), BF16),
            vmem((NX * NZL * NC, 16, count), BF16),
            vmem((bot, count), BF16),
            vmem((count, bot), BF16),
            vmem((1, count), F32),
            vmem((s_rows, bot), F32),
            vmem((s_rows, bot), BF16),
            vmem((bot, s_rows), BF16),
            vmem((s_rows, LANES), F32),
            vmem((t_rows, bot), BF16),
            vmem((s_rows, count), F32),
            vmem((t_rows, count), F32),
            vmem((s_pad, LANES), F32),
            vmem((t_pad, LANES), F32),
            vmem((s_pad + t_pad, LANES), F32),
            vmem((NY, 8, LANES), F32),
            vmem((NZH, 8, LANES), F32),
            vmem((s_rows, count), BF16),
            vmem((s_rows, bot), F32),
            vmem((2, ring, y_rows, bot), BF16),
            vmem((2, ring, y_rows, bot), BF16),
            vmem((NZH, z_rows, bot), F32),
            vmem((NZH, z_rows, bot), BF16),
            vmem((NZH, z_rows, bot), BF16),
            vmem((NY, NZH, z_rows, bot), BF16),
            vmem((NX * NZL, NC, 16, count), F32),
            vmem((NX * NZL, 16, count), BF16),
            vmem((NX * NZL, 16, count), BF16),
            vmem((2, NZL, short, 16, count), BF16),
            vmem((2, NZL, short, 16, count), BF16),
            vmem((NZL, 16, count), F32),
            vmem((NZL, 16, count), BF16),
            vmem((NZL, 16, count), BF16),
            pltpu.SemaphoreType.DMA((copies,)),
            pltpu.SemaphoreType.DMA((copies,)),
        ],
        compiler_params=pltpu.CompilerParams(
            collective_id=0, has_side_effects=True, vmem_limit_bytes=56 * 1024 * 1024
        ),
    )(pack, proto, teacher, center)


def body(student_feat, teacher_feat, student_proto, teacher_proto, center):
    s_rows, t_rows = student_feat.shape[0], teacher_feat.shape[0]
    t_pad = up(t_rows, LANES)
    width = max(s_rows, 3 * t_pad)
    student_t, teacher_t = student_feat.T, teacher_feat.T
    pieces = [jnp.pad(teacher_t[4 * q : 4 * q + 4], ((0, 0), (0, t_pad - t_rows))) for q in range(3)]
    pieces = jnp.concatenate(pieces, axis=1)
    pack = jnp.concatenate(
        [
            jnp.pad(student_t, ((0, 0), (0, width - s_rows))),
            jnp.pad(pieces, ((0, 0), (0, width - 3 * t_pad))),
        ],
        axis=0,
    )
    own_count = teacher_proto.shape[0]
    student_own = lax.dynamic_slice_in_dim(
        student_proto, lax.axis_index("dp") * own_count, own_count, 0
    ).astype(F32)
    new_teacher = MOMENTUM * teacher_proto + (1.0 - MOMENTUM) * student_own
    feat, raw = call(pack, student_proto, teacher_proto, center.reshape(1, -1), s_rows, t_rows)
    return (new_teacher, feat.astype(F32), raw)


def solution(mesh):
    placed = (P("dp", "fsdp"), P("dp", "fsdp"), P(None, "fsdp"), P("dp", "fsdp"), P("fsdp"))
    return jax.shard_map(
        body,
        mesh=mesh,
        in_specs=placed,
        out_specs=(P("dp", "fsdp"), P("dp", None), P("dp", "fsdp")),
        check_vma=False,
    )
```

```python
import functools

import jax
import jax.numpy as jnp
from jax import lax
from jax.experimental import pallas as pl
from jax.experimental.pallas import tpu as pltpu
from jax.sharding import PartitionSpec as P

NX, NZL, NC = 4, 3, 2
NY, NZH = 8, 4
STUDENT_CROPS = 8
GLOBAL_CROPS = 2
PROTO = 65536
EPSILON = 1e-06
MOMENTUM = 0.994
TEACHER_TEMP = 0.04
STUDENT_TEMP = 0.1
LANES = 128
COLS = 256
MESH = pl.DeviceIdType.MESH
F32 = jnp.float32
BF16 = jnp.bfloat16


def up(value, unit):
    return -(-value // unit) * unit


def hops(members, odd):
    long, short = members // 2, (members - 1) // 2
    return (short, long) if odd else (long, short)


class Spread:
    def __init__(self, send, spot, to, size, odd):
        self.send, self.spot, self.to = send, spot, to
        self.reach = dict(zip((1, -1), hops(size, odd)))
        self.out = {}

    def first(self):
        for way in (1, -1):
            for s in range(min(2, self.reach[way]), 0, -1):
                self.out[way, s] = self.send(self.spot(0), self.spot(0), self.to(way * s))

    def second(self):
        for way in (1, -1):
            if self.reach[way] > 2:
                self.out[way, 2].wait_recv()
                block = self.spot(-2 * way)
                for s in range(self.reach[way] - 2, 0, -1):
                    self.out[way, s + 2] = self.send(block, block, self.to(way * s))

    def arrivals(self):
        for way in (1, -1):
            for s in range(1, self.reach[way] + 1):
                if not (s == 2 and self.reach[way] > 2):
                    yield self.out[way, s], self.spot(-way * s)

    def last(self):
        for copy, _ in self.arrivals():
            copy.wait_recv()


class Gathered:
    def __init__(self, send, own, wire, land, to, size, odd):
        self.send, self.own, self.wire, self.land, self.to = send, own, wire, land, to
        self.reach = dict(zip((1, -1), hops(size, odd)))
        self.out = {}

    def post(self, way, kind, value, steps):
        side = 0 if way == 1 else 1
        self.wire[side, kind] = value.astype(self.wire.dtype)
        self.out[way, kind] = self.send(
            self.wire.at[side, kind], self.land.at[side, kind], self.to(way * steps)
        )

    def took(self, way, kind):
        self.out[way, kind].wait_recv()
        return self.land[0 if way == 1 else 1, kind].astype(F32)

    def first(self):
        for way in (1, -1):
            if self.reach[way] > 3:
                self.post(way, 3, self.own(4 * way), 2)
        for way in (1, -1):
            if self.reach[way] > 2:
                self.post(way, 2, self.own(3 * way), 1)
        for way in (1, -1):
            if self.reach[way] > 0:
                self.post(way, 0, self.own(way), 1)

    def second(self):
        for way in (1, -1):
            if self.reach[way] > 1:
                value = self.own(2 * way)
                for kind in (2, 3):
                    if self.reach[way] > kind:
                        value = value + self.took(way, kind)
                self.post(way, 1, value, 2)

    def total(self):
        value = self.own(0)
        for kind in (0, 1):
            for way in (1, -1):
                if self.reach[way] > kind:
                    value = value + self.took(way, kind)
        return value


def kernel(
    pack_ref, proto_ref, teacher_ref, center_ref, new_ref, feat_ref, raw_ref,
    norm_near, norm_x, feats, masters, half, half_t, proto_inv, unit, rows, rows_t, row_inv,
    t_rows, s_exp, t_exp, s_sum, t_sum, scale, den_y, den_z, grads, s_part, t_part,
    s_wire, s_land, t_wire, t_land, s_chunk, s_wire_z, s_land_z, t_chunk, t_land_z, final,
    raw, wire_c, land_c, wire_x, land_x, own_x, wire_l, land_l,
    send_sem, recv_sem,
):
    d, f = lax.axis_index("dp"), lax.axis_index("fsdp")
    c, zl, x = lax.rem(d, NC), lax.rem(d // NC, NZL), d // (NC * NZL)
    y, zh = f // NZH, lax.rem(f, NZH)
    bot, count = proto_ref.shape
    s_rows = unit.shape[0]
    t_pad = t_sum.shape[0]
    width = pack_ref.shape[1]
    tiles = count // COLS
    s_tiles, t_tiles = s_sum.shape[0] // LANES, t_pad // LANES
    share = s_rows // (NY * NZH)
    images = share // STUDENT_CROPS
    t_used = NY * NZH * 8

    def at(x_=x, zl_=zl, c_=c, y_=y, zh_=zh):
        return ((x_ * NZL + zl_) * NC + c_, y_ * NZH + zh_)

    def wrap(value, size):
        return lax.rem(value + size, size)

    def to_y(s):
        return at(y_=wrap(y + s, NY))

    def to_x(s):
        return at(x_=wrap(x + s, NX))

    def to_zh(k):
        return at(zh_=wrap(zh + k, NZH))

    def to_zl(k):
        return at(zl_=wrap(zl + k, NZL))

    used = [0]
    started = []

    def send(src, dst, to):
        i = used[0]
        used[0] += 1
        copy = pltpu.make_async_remote_copy(
            src_ref=src, dst_ref=dst, send_sem=send_sem.at[i], recv_sem=recv_sem.at[i],
            device_id=to, device_id_type=MESH,
        )
        copy.start()
        started.append(copy)
        return copy

    near = [
        at(zl_=wrap(zl + k, NZL), c_=lax.rem(c + e, NC))
        for k in range(NZL)
        for e in range(NC)
        if k or e
    ]
    partners = (
        [to_y(k) for k in range(1, NY)]
        + [to_zh(k) for k in range(1, NZH)]
        + near
        + [to_x(k) for k in range(1, NX)]
    )
    barrier = pltpu.get_barrier_semaphore()
    for partner in partners:
        pl.semaphore_signal(barrier, inc=1, device_id=partner, device_id_type=MESH)

    feats[y, zh] = pack_ref[...]
    student_own = proto_ref[pl.ds(pl.multiple_of(d * 16, 16), 16), :].astype(F32)
    own_master = MOMENTUM * teacher_ref[...] + (1.0 - MOMENTUM) * student_own
    new_ref[...] = own_master
    squares = jnp.sum(own_master * own_master, axis=0, keepdims=True)
    line = lax.broadcasted_iota(jnp.int32, (8, count // 8), 0)
    folded = jnp.zeros((8, count // 8), F32)
    for i in range(8):
        folded = jnp.where(line == i, squares[:, i * (count // 8) : (i + 1) * (count // 8)], folded)
    norm_near[0] = folded
    pl.semaphore_wait(barrier, len(partners))
    norms = [send(norm_near.at[0], norm_near.at[i + 1], to) for i, to in enumerate(near)]

    def along_z(buffer):
        return [send(buffer.at[y, zh], buffer.at[y, zh], to_zh(k)) for k in range(1, NZH)]

    def along_y(buffer):
        def spot_of(k):
            return lambda dy: buffer.at[wrap(y + dy, NY), wrap(zh - k, NZH)]

        return [Spread(send, spot_of(k), to_y, NY, k % 2) for k in range(NZH)]

    order = sorted(range(1, NZH), key=lambda k: (min(k, NZH - k), k))
    feat_z = along_z(feats)
    feat_y = along_y(feats)
    feat_y[0].first()

    @pl.loop(0, tiles)
    def _(n):
        at_n = pl.ds(pl.multiple_of(n * COLS, COLS), COLS)
        block = proto_ref[:, at_n].astype(F32)
        inverse = lax.rsqrt(jnp.sum(block * block, axis=0, keepdims=True) + EPSILON)
        normed = block * inverse
        half[:, at_n] = normed.astype(BF16)
        half_t[at_n, :] = normed.T.astype(BF16)
        proto_inv[:, at_n] = inverse

    for copy in norms:
        copy.wait_recv()
    norm_x[0] = jnp.sum(norm_near[...], axis=0)
    norms = [send(norm_x.at[0], norm_x.at[k], to_x(k)) for k in range(1, NX)]
    feat_y[0].second()
    for k in order:
        feat_z[k - 1].wait_recv()
        feat_y[k].first()
    for copy in norms:
        copy.wait_recv()
    inverse = lax.rsqrt(jnp.sum(norm_x[...], axis=0) + EPSILON)
    inverse = jnp.concatenate([inverse[i : i + 1] for i in range(8)], axis=1)
    masters[d] = (own_master * inverse).astype(BF16)

    across = []

    def to_sibling(block):
        across.append(send(block, block, at(c_=1 - c)))

    def master_of(k):
        return lambda dx: masters.at[(wrap(x + dx, NX) * NZL + wrap(zl - k, NZL)) * NC + c]

    master_z = [send(masters.at[d], masters.at[d], to_zl(k)) for k in range(1, NZL)]
    master_x = [Spread(send, master_of(k), to_x, NX, k % 2) for k in range(NZL)]
    master_x[0].first()
    to_sibling(masters.at[d])
    for k in order:
        feat_y[k].second()
    for k in range(1, NZL):
        master_z[k - 1].wait_recv()
        master_x[k].first()
        to_sibling(master_of(k)(0))
    for one in feat_y:
        one.last()
    for copy, block in master_x[0].arrivals():
        copy.wait_recv()
        to_sibling(block)

    slots = feats[...].reshape(NY * NZH * 16, width)
    spots = lax.broadcasted_iota(jnp.int32, (bot, NY * NZH * 16), 1)
    wanted = lax.broadcasted_iota(jnp.int32, (bot, NY * NZH * 16), 0)
    owner = lax.shift_right_logical(wanted * 5462, 16)
    pick_s = (spots == owner * 16 + (wanted - owner * 12)).astype(F32).astype(BF16)
    pick_t = (spots == owner * 16 + 12 + (wanted & 3)).astype(F32).astype(BF16)
    student_t = jnp.dot(pick_s, slots[:, :s_rows], preferred_element_type=F32)
    inverse = lax.rsqrt(jnp.sum(student_t * student_t, axis=0, keepdims=True) + EPSILON)
    rows_t[...] = (student_t * inverse).astype(BF16)
    student = student_t.T
    inverse = lax.rsqrt(jnp.sum(student * student, axis=1, keepdims=True) + EPSILON)
    normed = student * inverse
    unit[...] = normed
    rows[...] = normed.astype(BF16)
    row_inv[...] = jnp.broadcast_to(inverse, row_inv.shape)
    pieces = jnp.dot(pick_t, slots[:, : 3 * t_pad], preferred_element_type=F32)
    place = lax.broadcasted_iota(jnp.int32, (bot, t_pad), 0)
    owner = lax.shift_right_logical(place * 5462, 16)
    quarter = lax.shift_right_logical(place - owner * 12, 2)
    teacher_t = jnp.where(
        quarter == 0,
        pieces[:, :t_pad],
        jnp.where(quarter == 1, pieces[:, t_pad : 2 * t_pad], pieces[:, 2 * t_pad :]),
    )
    teacher = teacher_t.T
    inverse = lax.rsqrt(jnp.sum(teacher * teacher, axis=1, keepdims=True) + EPSILON)
    to_row = lax.broadcasted_iota(jnp.int32, (t_pad, t_pad), 0)
    from_row = lax.broadcasted_iota(jnp.int32, (t_pad, t_pad), 1)
    place = to_row & 7
    moved = (from_row == lax.shift_right_logical(to_row, 3) * (2 * images) + place) & (place < 2 * images)
    t_rows[...] = jnp.dot(
        moved.astype(F32).astype(BF16), (teacher * inverse).astype(BF16), preferred_element_type=F32
    ).astype(BF16)

    def fold(values):
        return values[:, :LANES] + values[:, LANES:]

    s_sum[...] = jnp.zeros_like(s_sum)
    t_sum[...] = jnp.zeros_like(t_sum)
    s_part[...] = jnp.zeros_like(s_part)
    t_part[...] = jnp.zeros_like(t_part)

    @pl.loop(0, tiles)
    def _(n):
        at_n = pl.ds(pl.multiple_of(n * COLS, COLS), COLS)
        logits = jnp.dot(rows[...], half[:, at_n], preferred_element_type=F32)
        value = jnp.exp(logits * (1.0 / STUDENT_TEMP))
        s_exp[:, at_n] = value
        s_sum[:s_rows, :] += fold(value)
        s_part[...] += jnp.dot(value.astype(BF16), half_t[at_n, :], preferred_element_type=F32)

    part = s_part[...]
    s_part[...] = part - unit[...] * jnp.sum(unit[...] * part, axis=1, keepdims=True)

    y_rows = s_rows // NY
    piece = y_rows // 2

    def own_s(h):
        def own(dy):
            start = wrap(y + dy, NY) * y_rows + h * piece
            return s_part[pl.ds(pl.multiple_of(start, 8), piece), :]

        return own

    s_ring = [
        Gathered(send, own_s(h), s_wire.at[h], s_land.at[h], to_y, NY, h) for h in range(2)
    ]
    for one in s_ring:
        one.first()
    for k in range(1, NZL):
        for copy, block in master_x[k].arrivals():
            copy.wait_recv()
            to_sibling(block)
    for copy in across:
        copy.wait_recv()

    @pl.loop(0, tiles)
    def _(n):
        at_n = pl.ds(pl.multiple_of(n * COLS, COLS), COLS)
        block = masters[:, :, at_n].reshape(bot, COLS)
        logits = jnp.dot(t_rows[...], block, preferred_element_type=F32)
        value = jnp.exp((logits - center_ref[:, at_n]) * (1.0 / TEACHER_TEMP))
        t_exp[:, at_n] = value
        t_sum[...] += fold(value)
        t_part[...] += jnp.dot(value.astype(BF16), half_t[at_n, :], preferred_element_type=F32)

    def own_t(dy):
        return t_part[pl.ds(pl.multiple_of(wrap(y + dy, NY) * (8 * NZH), 8), 8 * NZH), :]

    t_ring = Gathered(send, own_t, t_wire, t_land, to_y, NY, 1)
    t_ring.first()
    line = lax.broadcasted_iota(jnp.int32, (8, LANES), 0)
    packed = jnp.zeros((8, LANES), F32)
    for i in range(s_tiles + t_tiles):
        block = (
            s_sum[i * LANES : (i + 1) * LANES, :]
            if i < s_tiles
            else t_sum[(i - s_tiles) * LANES : (i - s_tiles + 1) * LANES, :]
        )
        packed = jnp.where(line == i, jnp.sum(block.T, axis=0, keepdims=True), packed)
    den_y[0] = packed
    dens = [send(den_y.at[0], den_y.at[k], to_y(k)) for k in range(1, NY)]
    for one in s_ring:
        one.second()
    t_ring.second()
    for copy in dens:
        copy.wait_recv()
    den_z[0] = jnp.sum(den_y[...], axis=0)
    dens = [send(den_z.at[0], den_z.at[k], to_zh(k)) for k in range(1, NZH)]
    s_chunk[...] = jnp.concatenate([one.total() for one in s_ring], axis=0).reshape(s_chunk.shape)
    s_met = []
    for k in range(1, NZH):
        s_wire_z[k] = s_chunk[wrap(zh + k, NZH)].astype(BF16)
        s_met.append(send(s_wire_z.at[k], s_land_z.at[k], to_zh(k)))
    t_chunk[...] = t_ring.total().reshape(t_chunk.shape)
    t_met = [
        send(t_chunk.at[wrap(zh + k, NZH)], t_land_z.at[k], to_zh(k)) for k in range(1, NZH)
    ]
    for copy in dens:
        copy.wait_recv()
    total = jnp.sum(den_z[...], axis=0)
    inverse = (PROTO / 16.0 / STUDENT_TEMP) / jnp.where(total > 0.0, total, 1.0)
    crop = lax.broadcasted_iota(jnp.int32, (LANES, LANES), 0) & (STUDENT_CROPS - 1)
    copies = jnp.where(crop < GLOBAL_CROPS, F32(GLOBAL_CROPS - 1), F32(GLOBAL_CROPS))
    for i in range(s_tiles + t_tiles):
        block = jnp.broadcast_to(inverse[i : i + 1, :], (LANES, LANES)).T
        scale[i * LANES : (i + 1) * LANES, :] = block * copies if i < s_tiles else block

    def partner_of(prob, i, position):
        first, second = prob[2 * i : 2 * i + 1], prob[2 * i + 1 : 2 * i + 2]
        return jnp.where(position == 0, second, jnp.where(position == 1, first, first + second))

    position = lax.broadcasted_iota(jnp.int32, (STUDENT_CROPS, count), 0)

    @pl.loop(0, NY * NZH // 2)
    def _(i):
        out = []
        for e in range(2):
            g = i * 2 + e
            at_t = pl.ds(pl.multiple_of(g * 8, 8), 8)
            at_s = pl.ds(pl.multiple_of(g * share, 8), share)
            t_scale = scale[pl.ds(pl.multiple_of(s_tiles * LANES + g * 8, 8), 8), :1]
            prob = t_exp[at_t, :] * t_scale
            value = s_exp[at_s, :] * scale[at_s, :1]
            for a in range(images):
                out.append(value[8 * a : 8 * a + 8] - partner_of(prob, a, position))
        both = pl.ds(pl.multiple_of(i * 2 * share, 16), 2 * share)
        grads[both, :] = jnp.concatenate(out, axis=0).astype(BF16)

    @pl.loop(0, tiles)
    def _(n):
        at_n = pl.ds(pl.multiple_of(n * COLS, COLS), COLS)
        part = jnp.dot(rows_t[...], grads[:, at_n], preferred_element_type=F32)
        inverse = proto_inv[:, at_n]
        normed = proto_ref[:, at_n].astype(F32) * inverse
        along = jnp.sum(normed * part, axis=0, keepdims=True)
        part = inverse * (part - normed * along)
        raw[:, :, :, at_n] = part.reshape(NX * NZL, NC, 16, COLS)
        wire_c[:, :, at_n] = raw[:, pl.ds(1 - c, 1), :, at_n].reshape(NX * NZL, 16, COLS).astype(BF16)

    over = []
    for k in sorted(range(NX), key=lambda k: -min(k, NX - k)):
        at_k = pl.ds(wrap(x + k, NX) * NZL, NZL)
        over.append(send(wire_c.at[at_k], land_c.at[at_k], at(c_=1 - c)))

    s_value, t_value = s_chunk[zh], t_chunk[zh]
    for k in range(1, NZH):
        s_met[k - 1].wait_recv()
        t_met[k - 1].wait_recv()
        s_value = s_value + s_land_z[k].astype(F32)
        t_value = t_value + t_land_z[k]
    at_s = pl.ds(pl.multiple_of(f * share, 8), share)
    s_value = s_value * scale[at_s, :1]
    t_value = t_value * scale[pl.ds(pl.multiple_of(s_tiles * LANES + f * 8, 8), 8), :1]
    position = lax.broadcasted_iota(jnp.int32, (STUDENT_CROPS, bot), 0)
    value = s_value - jnp.concatenate(
        [partner_of(t_value, a, position) for a in range(images)], axis=0
    )
    normed = unit[at_s, :]
    value = value - normed * jnp.sum(normed * value, axis=1, keepdims=True)
    final[y, zh] = (value * row_inv[at_s, :1]).astype(BF16)
    final_z = along_z(final)
    final_y = along_y(final)
    final_y[0].first()

    for copy in over:
        copy.wait_recv()

    def own_raw(k):
        def own(dx):
            slot = wrap(x + dx, NX) * NZL + k
            return raw[slot, c] + land_c[slot].astype(F32)

        return own

    raw_x = [
        Gathered(send, own_raw(k), wire_x.at[k], land_x.at[k], to_x, NX, k % 2) for k in range(NZL)
    ]
    for one in raw_x:
        one.first()
        one.second()
    final_y[0].second()
    for k in order:
        final_z[k - 1].wait_recv()
        final_y[k].first()
    for k in range(NZL):
        own_x[k] = raw_x[k].total()
    raw_met = []
    for k in range(1, NZL):
        wire_l[k] = own_x[wrap(zl + k, NZL)].astype(BF16)
        raw_met.append(send(wire_l.at[k], land_l.at[k], to_zl(k)))
    for k in order:
        final_y[k].second()
    value = own_x[zl]
    for k in range(1, NZL):
        raw_met[k - 1].wait_recv()
        value = value + land_l[k].astype(F32)
    raw_ref[...] = value
    for one in final_y:
        one.last()
    for i in range(NY):
        feat_ref[i * y_rows : (i + 1) * y_rows, :] = final[i].astype(F32).reshape(y_rows, bot)

    for copy in started:
        copy.wait_send()


def call(pack, proto, teacher, center, s_rows, t_rows):
    bot, count = proto.shape
    y_rows = s_rows // NY
    z_rows = y_rows // NZH
    width = pack.shape[1]
    vmem = pltpu.VMEM
    s_pad, t_pad = up(s_rows, LANES), up(t_rows, LANES)
    copies = (
        (NZL * NC - 1) + (NX - 1) + (NZH - 1) + NZH * (NY - 1)
        + (NZL - 1) + NZL * (NX - 1) + NZL * NX
        + (NY - 1) + (NZH - 1)
        + 3 * (NY - 1) + 2 * (NZH - 1) + (NZH - 1) + NZH * (NY - 1)
        + NX + NZL * (NX - 1) + (NZL - 1)
    )
    return pl.pallas_call(
        kernel,
        out_shape=(
            jax.ShapeDtypeStruct((16, count), F32),
            jax.ShapeDtypeStruct((s_rows, bot), F32),
            jax.ShapeDtypeStruct((16, count), F32),
        ),
        in_specs=[pl.BlockSpec(memory_space=pltpu.VMEM)] * 4,
        out_specs=[pl.BlockSpec(memory_space=pltpu.VMEM)] * 3,
        scratch_shapes=[
            vmem((NZL * NC, 8, count // 8), F32),
            vmem((NX, 8, count // 8), F32),
            vmem((NY, NZH, 16, width), BF16),
            vmem((NX * NZL * NC, 16, count), BF16),
            vmem((bot, count), BF16),
            vmem((count, bot), BF16),
            vmem((1, count), F32),
            vmem((s_rows, bot), F32),
            vmem((s_rows, bot), BF16),
            vmem((bot, s_rows), BF16),
            vmem((s_rows, LANES), F32),
            vmem((t_pad, bot), BF16),
            vmem((s_rows, count), F32),
            vmem((t_pad, count), F32),
            vmem((s_pad, LANES), F32),
            vmem((t_pad, LANES), F32),
            vmem((s_pad + t_pad, LANES), F32),
            vmem((NY, 8, LANES), F32),
            vmem((NZH, 8, LANES), F32),
            vmem((s_rows, count), BF16),
            vmem((s_rows, bot), F32),
            vmem((t_pad, bot), F32),
            vmem((2, 2, 4, y_rows // 2, bot), BF16),
            vmem((2, 2, 4, y_rows // 2, bot), BF16),
            vmem((2, 4, 8 * NZH, bot), F32),
            vmem((2, 4, 8 * NZH, bot), F32),
            vmem((NZH, z_rows, bot), F32),
            vmem((NZH, z_rows, bot), BF16),
            vmem((NZH, z_rows, bot), BF16),
            vmem((NZH, 8, bot), F32),
            vmem((NZH, 8, bot), F32),
            vmem((NY, NZH, z_rows, bot), BF16),
            vmem((NX * NZL, NC, 16, count), F32),
            vmem((NX * NZL, 16, count), BF16),
            vmem((NX * NZL, 16, count), BF16),
            vmem((NZL, 2, 4, 16, count), BF16),
            vmem((NZL, 2, 4, 16, count), BF16),
            vmem((NZL, 16, count), F32),
            vmem((NZL, 16, count), BF16),
            vmem((NZL, 16, count), BF16),
            pltpu.SemaphoreType.DMA((copies,)),
            pltpu.SemaphoreType.DMA((copies,)),
        ],
        compiler_params=pltpu.CompilerParams(
            collective_id=0, has_side_effects=True, vmem_limit_bytes=56 * 1024 * 1024
        ),
    )(pack, proto, teacher, center)


def body(student_feat, teacher_feat, student_proto, teacher_proto, center):
    s_rows, t_rows = student_feat.shape[0], teacher_feat.shape[0]
    t_pad = up(t_rows, LANES)
    width = max(s_rows, 3 * t_pad)
    student_t, teacher_t = student_feat.T, teacher_feat.T
    pieces = [jnp.pad(teacher_t[4 * q : 4 * q + 4], ((0, 0), (0, t_pad - t_rows))) for q in range(3)]
    pieces = jnp.concatenate(pieces, axis=1)
    pack = jnp.concatenate(
        [
            jnp.pad(student_t, ((0, 0), (0, width - s_rows))),
            jnp.pad(pieces, ((0, 0), (0, width - 3 * t_pad))),
        ],
        axis=0,
    )
    return tuple(call(pack, student_proto, teacher_proto, center.reshape(1, -1), s_rows, t_rows))


def solution(mesh):
    placed = (P("dp", "fsdp"), P("dp", "fsdp"), P(None, "fsdp"), P("dp", "fsdp"), P("fsdp"))
    return jax.shard_map(
        body,
        mesh=mesh,
        in_specs=placed,
        out_specs=(P("dp", "fsdp"), P("dp", None), P("dp", "fsdp")),
        check_vma=False,
    )
```

```python
import functools

import jax
import jax.numpy as jnp
from jax import lax
from jax.experimental import pallas as pl
from jax.experimental.pallas import tpu as pltpu
from jax.sharding import PartitionSpec as P

NX, NZL, NC = 4, 3, 2
NY, NZH = 8, 4
STUDENT_CROPS = 8
GLOBAL_CROPS = 2
PROTO = 65536
EPSILON = 1e-06
MOMENTUM = 0.994
TEACHER_TEMP = 0.04
STUDENT_TEMP = 0.1
LANES = 128
COLS = 256
MESH = pl.DeviceIdType.MESH
F32 = jnp.float32
BF16 = jnp.bfloat16


def up(value, unit):
    return -(-value // unit) * unit


def hops(members, odd):
    long, short = members // 2, (members - 1) // 2
    return (short, long) if odd else (long, short)


class Spread:
    def __init__(self, send, spot, to, size, odd, straight=2):
        self.send, self.spot, self.to, self.straight = send, spot, to, straight
        self.reach = dict(zip((1, -1), hops(size, odd)))
        self.out = {}

    def first(self):
        for way in (1, -1):
            for s in range(min(self.straight, self.reach[way]), 0, -1):
                self.out[way, s] = self.send(self.spot(0), self.spot(0), self.to(way * s))

    def second(self):
        for way in (1, -1):
            if self.reach[way] > self.straight:
                self.out[way, 2].wait_recv()
                block = self.spot(-2 * way)
                for s in range(self.reach[way] - 2, 0, -1):
                    self.out[way, s + 2] = self.send(block, block, self.to(way * s))

    def arrivals(self):
        for way in (1, -1):
            for s in range(1, self.reach[way] + 1):
                if not (s == 2 and self.reach[way] > self.straight):
                    yield self.out[way, s], self.spot(-way * s)

    def last(self):
        for copy, _ in self.arrivals():
            copy.wait_recv()


class Gathered:
    def __init__(self, send, own, wire, land, to, size, odd):
        self.send, self.own, self.wire, self.land, self.to = send, own, wire, land, to
        self.reach = dict(zip((1, -1), hops(size, odd)))
        self.out = {}

    def post(self, way, kind, value, steps):
        side = 0 if way == 1 else 1
        self.wire[side, kind] = value.astype(self.wire.dtype)
        self.out[way, kind] = self.send(
            self.wire.at[side, kind], self.land.at[side, kind], self.to(way * steps)
        )

    def took(self, way, kind):
        self.out[way, kind].wait_recv()
        return self.land[0 if way == 1 else 1, kind].astype(F32)

    def first(self):
        for way in (1, -1):
            if self.reach[way] > 3:
                self.post(way, 3, self.own(4 * way), 2)
        for way in (1, -1):
            if self.reach[way] > 2:
                self.post(way, 2, self.own(3 * way), 1)
        for way in (1, -1):
            if self.reach[way] > 0:
                self.post(way, 0, self.own(way), 1)

    def second(self):
        for way in (1, -1):
            if self.reach[way] > 1:
                value = self.own(2 * way)
                for kind in (2, 3):
                    if self.reach[way] > kind:
                        value = value + self.took(way, kind)
                self.post(way, 1, value, 2)

    def total(self):
        value = self.own(0)
        for kind in (0, 1):
            for way in (1, -1):
                if self.reach[way] > kind:
                    value = value + self.took(way, kind)
        return value


def kernel(
    student_ref, teacher_feat_ref, proto_ref, teacher_ref, center_ref, new_ref, feat_ref, raw_ref,
    feats, masters, half, half_t, proto_inv, unit, rows, rows_t, row_inv,
    t_rows, s_exp, t_exp, s_sum, t_sum, scale, den_y, den_z, grads, s_part, t_part,
    s_wire, s_land, t_wire, t_land, s_chunk, s_wire_z, s_land_z, t_chunk, t_land_z, final,
    raw, wire_c, land_c, wire_x, land_x, own_x, wire_l, land_l,
    send_sem, recv_sem,
):
    d, f = lax.axis_index("dp"), lax.axis_index("fsdp")
    c, zl, x = lax.rem(d, NC), lax.rem(d // NC, NZL), d // (NC * NZL)
    y, zh = f // NZH, lax.rem(f, NZH)
    bot, count = proto_ref.shape
    s_rows = unit.shape[0]
    t_pad = t_sum.shape[0]
    width = feats.shape[3]
    tiles = count // COLS
    s_tiles, t_tiles = s_sum.shape[0] // LANES, t_pad // LANES
    share = s_rows // (NY * NZH)
    images = share // STUDENT_CROPS
    t_used = NY * NZH * 8

    def at(x_=x, zl_=zl, c_=c, y_=y, zh_=zh):
        return ((x_ * NZL + zl_) * NC + c_, y_ * NZH + zh_)

    def wrap(value, size):
        return lax.rem(value + size, size)

    def to_y(s):
        return at(y_=wrap(y + s, NY))

    def to_x(s):
        return at(x_=wrap(x + s, NX))

    def to_zh(k):
        return at(zh_=wrap(zh + k, NZH))

    def to_zl(k):
        return at(zl_=wrap(zl + k, NZL))

    used = [0]
    started = []

    def send(src, dst, to):
        i = used[0]
        used[0] += 1
        copy = pltpu.make_async_remote_copy(
            src_ref=src, dst_ref=dst, send_sem=send_sem.at[i], recv_sem=recv_sem.at[i],
            device_id=to, device_id_type=MESH,
        )
        copy.start()
        started.append(copy)
        return copy

    partners = (
        [to_y(k) for k in range(1, NY)]
        + [to_zh(k) for k in range(1, NZH)]
        + [to_zl(k) for k in range(1, NZL)]
        + [at(c_=1 - c)]
        + [to_x(k) for k in range(1, NX)]
    )
    barrier = pltpu.get_barrier_semaphore()
    for partner in partners:
        pl.semaphore_signal(barrier, inc=1, device_id=partner, device_id_type=MESH)

    teacher_feat = teacher_feat_ref[...].astype(F32)
    wide = [student_ref[...].astype(F32)]
    if width > s_rows:
        wide.append(jnp.zeros((12, width - s_rows), F32))
    slot = jnp.concatenate(
        [jnp.concatenate(wide, axis=1), jnp.zeros((4, width), F32)], axis=0
    )
    t_count = teacher_feat.shape[1]
    fill = [jnp.zeros((4, t_pad - t_count), F32)] if t_pad > t_count else []
    last = []
    for q in range(3):
        last += [teacher_feat[4 * q : 4 * q + 4]] + fill
    if width > 3 * t_pad:
        last.append(jnp.zeros((4, width - 3 * t_pad), F32))
    last = jnp.concatenate(last, axis=1)
    low = jnp.concatenate([jnp.zeros((4, width), F32), last], axis=0)
    line = lax.broadcasted_iota(jnp.int32, (16, width), 0)
    feats[y, zh] = jnp.where(
        line < 12, slot, jnp.concatenate([jnp.zeros((8, width), F32), low], axis=0)
    ).astype(BF16)
    student_own = proto_ref[pl.ds(pl.multiple_of(d * 16, 16), 16), :].astype(F32)
    own_master = MOMENTUM * teacher_ref[...] + (1.0 - MOMENTUM) * student_own
    new_ref[...] = own_master
    masters[d] = own_master
    pl.semaphore_wait(barrier, len(partners))

    def along_z(buffer):
        return [send(buffer.at[y, zh], buffer.at[y, zh], to_zh(k)) for k in range(1, NZH)]

    def along_y(buffer):
        def spot_of(k):
            return lambda dy: buffer.at[wrap(y + dy, NY), wrap(zh - k, NZH)]

        return [
            Spread(send, spot_of(k), to_y, NY, k % 2, NY if 2 * k == NZH else 2)
            for k in range(NZH)
        ]

    order = sorted(range(1, NZH), key=lambda k: (min(k, NZH - k), k))
    feat_z = along_z(feats)
    feat_y = along_y(feats)
    feat_y[0].first()

    across = []

    def to_sibling(block):
        across.append(send(block, block, at(c_=1 - c)))

    def master_of(k):
        return lambda dx: masters.at[(wrap(x + dx, NX) * NZL + wrap(zl - k, NZL)) * NC + c]

    master_z = [send(masters.at[d], masters.at[d], to_zl(k)) for k in range(1, NZL)]
    master_x = [Spread(send, master_of(k), to_x, NX, k % 2) for k in range(NZL)]
    master_x[0].first()
    to_sibling(masters.at[d])

    @pl.loop(0, tiles)
    def _(n):
        at_n = pl.ds(pl.multiple_of(n * COLS, COLS), COLS)
        block = proto_ref[:, at_n].astype(F32)
        inverse = lax.rsqrt(jnp.sum(block * block, axis=0, keepdims=True) + EPSILON)
        normed = block * inverse
        half[:, at_n] = normed.astype(BF16)
        half_t[at_n, :] = normed.T.astype(BF16)
        proto_inv[:, at_n] = inverse

    feat_y[0].second()
    for k in order:
        feat_z[k - 1].wait_recv()
        feat_y[k].first()
    for k in range(1, NZL):
        master_z[k - 1].wait_recv()
        master_x[k].first()
        to_sibling(master_of(k)(0))
    for k in order:
        feat_y[k].second()
    for copy, block in master_x[0].arrivals():
        copy.wait_recv()
        to_sibling(block)
    for one in feat_y:
        one.last()

    slots = feats[...].reshape(NY * NZH * 16, width)
    spots = lax.broadcasted_iota(jnp.int32, (bot, NY * NZH * 16), 1)
    wanted = lax.broadcasted_iota(jnp.int32, (bot, NY * NZH * 16), 0)
    owner = lax.shift_right_logical(wanted * 5462, 16)
    pick_s = (spots == owner * 16 + (wanted - owner * 12)).astype(F32).astype(BF16)
    pick_t = (spots == owner * 16 + 12 + (wanted & 3)).astype(F32).astype(BF16)
    student_t = jnp.dot(pick_s, slots[:, :s_rows], preferred_element_type=F32)
    inverse = lax.rsqrt(jnp.sum(student_t * student_t, axis=0, keepdims=True) + EPSILON)
    rows_t[...] = (student_t * inverse).astype(BF16)
    student = student_t.T
    inverse = lax.rsqrt(jnp.sum(student * student, axis=1, keepdims=True) + EPSILON)
    normed = student * inverse
    unit[...] = normed
    rows[...] = normed.astype(BF16)
    row_inv[...] = jnp.broadcast_to(inverse, row_inv.shape)
    pieces = jnp.dot(pick_t, slots[:, : 3 * t_pad], preferred_element_type=F32)
    place = lax.broadcasted_iota(jnp.int32, (bot, t_pad), 0)
    owner = lax.shift_right_logical(place * 5462, 16)
    quarter = lax.shift_right_logical(place - owner * 12, 2)
    teacher_t = jnp.where(
        quarter == 0,
        pieces[:, :t_pad],
        jnp.where(quarter == 1, pieces[:, t_pad : 2 * t_pad], pieces[:, 2 * t_pad :]),
    )
    teacher = teacher_t.T
    inverse = lax.rsqrt(jnp.sum(teacher * teacher, axis=1, keepdims=True) + EPSILON)
    to_row = lax.broadcasted_iota(jnp.int32, (t_pad, t_pad), 0)
    from_row = lax.broadcasted_iota(jnp.int32, (t_pad, t_pad), 1)
    place = to_row & 7
    moved = (from_row == lax.shift_right_logical(to_row, 3) * (2 * images) + place) & (place < 2 * images)
    t_rows[...] = jnp.dot(
        moved.astype(F32).astype(BF16), (teacher * inverse).astype(BF16), preferred_element_type=F32
    ).astype(BF16)

    def fold(values):
        return values[:, :LANES] + values[:, LANES:]

    s_sum[...] = jnp.zeros_like(s_sum)
    t_sum[...] = jnp.zeros_like(t_sum)
    s_part[...] = jnp.zeros_like(s_part)
    t_part[...] = jnp.zeros_like(t_part)

    def student_tile(n):
        at_n = pl.ds(pl.multiple_of(n * COLS, COLS), COLS)
        logits = jnp.dot(rows[...], half[:, at_n], preferred_element_type=F32)
        value = jnp.exp(logits * (1.0 / STUDENT_TEMP))
        s_exp[:, at_n] = value
        s_sum[:s_rows, :] += fold(value)
        s_part[...] += jnp.dot(value.astype(BF16), half_t[at_n, :], preferred_element_type=F32)

    def masters_on(k):
        for copy, block in master_x[k].arrivals():
            copy.wait_recv()
            to_sibling(block)

    early = tiles * 5 // 8
    pl.loop(0, early)(student_tile)
    if NZL > 1:
        masters_on(1)
    pl.loop(early, tiles)(student_tile)

    part = s_part[...]
    s_part[...] = part - unit[...] * jnp.sum(unit[...] * part, axis=1, keepdims=True)

    y_rows = s_rows // NY
    piece = y_rows // 2

    def own_s(h):
        def own(dy):
            start = wrap(y + dy, NY) * y_rows + h * piece
            return s_part[pl.ds(pl.multiple_of(start, 8), piece), :]

        return own

    s_ring = [
        Gathered(send, own_s(h), s_wire.at[h], s_land.at[h], to_y, NY, h) for h in range(2)
    ]
    for one in s_ring:
        one.first()
    for k in range(2, NZL):
        masters_on(k)
    for copy in across:
        copy.wait_recv()

    @pl.loop(0, tiles)
    def _(n):
        at_n = pl.ds(pl.multiple_of(n * COLS, COLS), COLS)
        block = masters[:, :, at_n].reshape(bot, COLS)
        inverse = lax.rsqrt(jnp.sum(block * block, axis=0, keepdims=True) + EPSILON)
        logits = jnp.dot(t_rows[...], (block * inverse).astype(BF16), preferred_element_type=F32)
        value = jnp.exp((logits - center_ref[:, at_n]) * (1.0 / TEACHER_TEMP))
        t_exp[:, at_n] = value
        t_sum[...] += fold(value)
        t_part[...] += jnp.dot(value.astype(BF16), half_t[at_n, :], preferred_element_type=F32)

    def own_t(dy):
        return t_part[pl.ds(pl.multiple_of(wrap(y + dy, NY) * (8 * NZH), 8), 8 * NZH), :]

    line = lax.broadcasted_iota(jnp.int32, (8, LANES), 0)
    packed = jnp.zeros((8, LANES), F32)
    for i in range(s_tiles + t_tiles):
        block = (
            s_sum[i * LANES : (i + 1) * LANES, :]
            if i < s_tiles
            else t_sum[(i - s_tiles) * LANES : (i - s_tiles + 1) * LANES, :]
        )
        packed = jnp.where(line == i, jnp.sum(block.T, axis=0, keepdims=True), packed)
    den_y[0] = packed
    dens = [send(den_y.at[0], den_y.at[k], to_y(k)) for k in range(1, NY)]
    t_ring = Gathered(send, own_t, t_wire, t_land, to_y, NY, 1)
    t_ring.first()
    for one in s_ring:
        one.second()
    t_ring.second()
    for copy in dens:
        copy.wait_recv()
    den_z[0] = jnp.sum(den_y[...], axis=0)
    dens = [send(den_z.at[0], den_z.at[k], to_zh(k)) for k in range(1, NZH)]
    s_chunk[...] = jnp.concatenate([one.total() for one in s_ring], axis=0).reshape(s_chunk.shape)
    s_met = []
    for k in range(1, NZH):
        s_wire_z[k] = s_chunk[wrap(zh + k, NZH)].astype(BF16)
        s_met.append(send(s_wire_z.at[k], s_land_z.at[k], to_zh(k)))
    t_chunk[...] = t_ring.total().reshape(t_chunk.shape)
    t_met = [
        send(t_chunk.at[wrap(zh + k, NZH)], t_land_z.at[k], to_zh(k)) for k in range(1, NZH)
    ]
    for copy in dens:
        copy.wait_recv()
    total = jnp.sum(den_z[...], axis=0)
    inverse = (PROTO / 16.0 / STUDENT_TEMP) / jnp.where(total > 0.0, total, 1.0)
    crop = lax.broadcasted_iota(jnp.int32, (LANES, LANES), 0) & (STUDENT_CROPS - 1)
    copies = jnp.where(crop < GLOBAL_CROPS, F32(GLOBAL_CROPS - 1), F32(GLOBAL_CROPS))
    for i in range(s_tiles + t_tiles):
        block = jnp.broadcast_to(inverse[i : i + 1, :], (LANES, LANES)).T
        scale[i * LANES : (i + 1) * LANES, :] = block * copies if i < s_tiles else block

    def partner_of(prob, i, position):
        first, second = prob[2 * i : 2 * i + 1], prob[2 * i + 1 : 2 * i + 2]
        return jnp.where(position == 0, second, jnp.where(position == 1, first, first + second))

    position = lax.broadcasted_iota(jnp.int32, (STUDENT_CROPS, count), 0)

    @pl.loop(0, NY * NZH // 2)
    def _(i):
        out = []
        for e in range(2):
            g = i * 2 + e
            at_t = pl.ds(pl.multiple_of(g * 8, 8), 8)
            at_s = pl.ds(pl.multiple_of(g * share, 8), share)
            t_scale = scale[pl.ds(pl.multiple_of(s_tiles * LANES + g * 8, 8), 8), :1]
            prob = t_exp[at_t, :] * t_scale
            value = s_exp[at_s, :] * scale[at_s, :1]
            for a in range(images):
                out.append(value[8 * a : 8 * a + 8] - partner_of(prob, a, position))
        both = pl.ds(pl.multiple_of(i * 2 * share, 16), 2 * share)
        grads[both, :] = jnp.concatenate(out, axis=0).astype(BF16)

    wide = count // 2

    def proto_tile(q):
        def tile(n):
            at_n = pl.ds(pl.multiple_of(n * COLS, COLS), COLS)
            at_q = pl.ds(pl.multiple_of(n * COLS - q * wide, COLS), COLS)
            part = jnp.dot(rows_t[...], grads[:, at_n], preferred_element_type=F32)
            inverse = proto_inv[:, at_n]
            normed = proto_ref[:, at_n].astype(F32) * inverse
            along = jnp.sum(normed * part, axis=0, keepdims=True)
            part = inverse * (part - normed * along)
            raw[q, :, :, :, at_q] = part.reshape(NX * NZL, NC, 16, COLS)
            wire_c[q, :, :, at_q] = (
                raw[q, :, pl.ds(1 - c, 1), :, at_q].reshape(NX * NZL, 16, COLS).astype(BF16)
            )

        return tile

    def own_raw(q, k):
        def own(dx):
            slot = wrap(x + dx, NX) * NZL + k
            return raw[q, slot, c] + land_c[q, slot].astype(F32)

        return own

    over = []
    raw_x = []
    for q in range(2):
        pl.loop(q * tiles // 2, (q + 1) * tiles // 2)(proto_tile(q))
        over.append(send(wire_c.at[q], land_c.at[q], at(c_=1 - c)))
        raw_x.append(
            [
                Gathered(
                    send, own_raw(q, k), wire_x.at[q, k], land_x.at[q, k], to_x, NX, (k + q) % 2
                )
                for k in range(NZL)
            ]
        )

    def on_x(q):
        over[q].wait_recv()
        for one in raw_x[q]:
            one.first()
            one.second()

    on_x(0)

    s_value, t_value = s_chunk[zh], t_chunk[zh]
    for k in range(1, NZH):
        s_met[k - 1].wait_recv()
        t_met[k - 1].wait_recv()
        s_value = s_value + s_land_z[k].astype(F32)
        t_value = t_value + t_land_z[k]
    at_s = pl.ds(pl.multiple_of(f * share, 8), share)
    s_value = s_value * scale[at_s, :1]
    t_value = t_value * scale[pl.ds(pl.multiple_of(s_tiles * LANES + f * 8, 8), 8), :1]
    position = lax.broadcasted_iota(jnp.int32, (STUDENT_CROPS, bot), 0)
    value = s_value - jnp.concatenate(
        [partner_of(t_value, a, position) for a in range(images)], axis=0
    )
    normed = unit[at_s, :]
    value = value - normed * jnp.sum(normed * value, axis=1, keepdims=True)
    final[y, zh] = (value * row_inv[at_s, :1]).astype(BF16)
    final_z = along_z(final)
    final_y = along_y(final)
    final_y[0].first()

    on_x(1)
    final_y[0].second()
    for k in order:
        final_z[k - 1].wait_recv()
        final_y[k].first()
    raw_met = []
    for q in range(2):
        for k in range(NZL):
            own_x[q, k] = raw_x[q][k].total()
        for k in range(1, NZL):
            wire_l[q, k] = own_x[q, wrap(zl + k, NZL)].astype(BF16)
            raw_met.append(send(wire_l.at[q, k], land_l.at[q, k], to_zl(k)))
        if q == 0:
            for k in order:
                final_y[k].second()
    for q in range(2):
        value = own_x[q, zl]
        for k in range(1, NZL):
            raw_met[q * (NZL - 1) + k - 1].wait_recv()
            value = value + land_l[q, k].astype(F32)
        raw_ref[:, q * wide : (q + 1) * wide] = value
    for one in final_y:
        one.last()
    for i in range(NY):
        feat_ref[i * y_rows : (i + 1) * y_rows, :] = final[i].astype(F32).reshape(y_rows, bot)

    for copy in started:
        copy.wait_send()


def call(student, teacher_feat, proto, teacher, center):
    bot, count = proto.shape
    s_rows, t_rows = student.shape[1], teacher_feat.shape[1]
    y_rows = s_rows // NY
    z_rows = y_rows // NZH
    vmem = pltpu.VMEM
    s_pad, t_pad = up(s_rows, LANES), up(t_rows, LANES)
    width = max(s_rows, 3 * t_pad)
    copies = (
        (NZH - 1) + NZH * (NY - 1)
        + (NZL - 1) + NZL * (NX - 1) + NZL * NX
        + (NY - 1) + (NZH - 1)
        + 3 * (NY - 1) + 2 * (NZH - 1) + (NZH - 1) + NZH * (NY - 1)
        + 2 + 2 * NZL * (NX - 1) + 2 * (NZL - 1)
    )
    return pl.pallas_call(
        kernel,
        out_shape=(
            jax.ShapeDtypeStruct((16, count), F32),
            jax.ShapeDtypeStruct((s_rows, bot), F32),
            jax.ShapeDtypeStruct((16, count), F32),
        ),
        in_specs=[pl.BlockSpec(memory_space=pltpu.VMEM)] * 5,
        out_specs=[pl.BlockSpec(memory_space=pltpu.VMEM)] * 3,
        scratch_shapes=[
            vmem((NY, NZH, 16, width), BF16),
            vmem((NX * NZL * NC, 16, count), F32),
            vmem((bot, count), BF16),
            vmem((count, bot), BF16),
            vmem((1, count), F32),
            vmem((s_rows, bot), F32),
            vmem((s_rows, bot), BF16),
            vmem((bot, s_rows), BF16),
            vmem((s_rows, LANES), F32),
            vmem((t_pad, bot), BF16),
            vmem((s_rows, count), F32),
            vmem((t_pad, count), F32),
            vmem((s_pad, LANES), F32),
            vmem((t_pad, LANES), F32),
            vmem((s_pad + t_pad, LANES), F32),
            vmem((NY, 8, LANES), F32),
            vmem((NZH, 8, LANES), F32),
            vmem((s_rows, count), BF16),
            vmem((s_rows, bot), F32),
            vmem((t_pad, bot), F32),
            vmem((2, 2, 4, y_rows // 2, bot), BF16),
            vmem((2, 2, 4, y_rows // 2, bot), BF16),
            vmem((2, 4, 8 * NZH, bot), F32),
            vmem((2, 4, 8 * NZH, bot), F32),
            vmem((NZH, z_rows, bot), F32),
            vmem((NZH, z_rows, bot), BF16),
            vmem((NZH, z_rows, bot), BF16),
            vmem((NZH, 8, bot), F32),
            vmem((NZH, 8, bot), F32),
            vmem((NY, NZH, z_rows, bot), BF16),
            vmem((2, NX * NZL, NC, 16, count // 2), F32),
            vmem((2, NX * NZL, 16, count // 2), BF16),
            vmem((2, NX * NZL, 16, count // 2), BF16),
            vmem((2, NZL, 2, 2, 16, count // 2), BF16),
            vmem((2, NZL, 2, 2, 16, count // 2), BF16),
            vmem((2, NZL, 16, count // 2), F32),
            vmem((2, NZL, 16, count // 2), BF16),
            vmem((2, NZL, 16, count // 2), BF16),
            pltpu.SemaphoreType.DMA((copies,)),
            pltpu.SemaphoreType.DMA((copies,)),
        ],
        compiler_params=pltpu.CompilerParams(
            collective_id=0, has_side_effects=True, vmem_limit_bytes=56 * 1024 * 1024
        ),
    )(student, teacher_feat, proto, teacher, center)


def body(student_feat, teacher_feat, student_proto, teacher_proto, center):
    return tuple(
        call(student_feat.T, teacher_feat.T, student_proto, teacher_proto, center.reshape(1, -1))
    )


def solution(mesh):
    placed = (P("dp", "fsdp"), P("dp", "fsdp"), P(None, "fsdp"), P("dp", "fsdp"), P("fsdp"))
    return jax.shard_map(
        body,
        mesh=mesh,
        in_specs=placed,
        out_specs=(P("dp", "fsdp"), P("dp", None), P("dp", "fsdp")),
        check_vma=False,
    )
```

```python
import functools

import jax
import jax.numpy as jnp
from jax import lax
from jax.experimental import pallas as pl
from jax.experimental.pallas import tpu as pltpu
from jax.sharding import PartitionSpec as P

NX, NZL, NC = 4, 3, 2
NY, NZH = 8, 4
STUDENT_CROPS = 8
GLOBAL_CROPS = 2
PROTO = 65536
EPSILON = 1e-06
MOMENTUM = 0.994
TEACHER_TEMP = 0.04
STUDENT_TEMP = 0.1
LANES = 128
COLS = 512
WIDE = 1024
MESH = pl.DeviceIdType.MESH
F32 = jnp.float32
BF16 = jnp.bfloat16


def up(value, unit):
    return -(-value // unit) * unit


def hops(members, odd):
    long, short = members // 2, (members - 1) // 2
    return (short, long) if odd else (long, short)


class Spread:
    def __init__(self, send, spot, to, size, odd, straight=2):
        self.send, self.spot, self.to, self.straight = send, spot, to, straight
        self.reach = dict(zip((1, -1), hops(size, odd)))
        self.out = {}

    def first(self):
        for way in (1, -1):
            for s in range(min(self.straight, self.reach[way]), 0, -1):
                self.out[way, s] = self.send(self.spot(0), self.spot(0), self.to(way * s))

    def second(self):
        for way in (1, -1):
            if self.reach[way] > self.straight:
                self.out[way, 2].wait_recv()
                block = self.spot(-2 * way)
                for s in range(self.reach[way] - 2, 0, -1):
                    self.out[way, s + 2] = self.send(block, block, self.to(way * s))

    def arrivals(self):
        for way in (1, -1):
            for s in range(1, self.reach[way] + 1):
                if not (s == 2 and self.reach[way] > self.straight):
                    yield self.out[way, s], self.spot(-way * s)

    def last(self):
        for copy, _ in self.arrivals():
            copy.wait_recv()


class Gathered:
    def __init__(self, send, own, wire, land, to, size, odd):
        self.send, self.own, self.wire, self.land, self.to = send, own, wire, land, to
        self.reach = dict(zip((1, -1), hops(size, odd)))
        self.out = {}

    def post(self, way, kind, value, steps):
        side = 0 if way == 1 else 1
        self.wire[side, kind] = value.astype(self.wire.dtype)
        self.out[way, kind] = self.send(
            self.wire.at[side, kind], self.land.at[side, kind], self.to(way * steps)
        )

    def took(self, way, kind):
        self.out[way, kind].wait_recv()
        return self.land[0 if way == 1 else 1, kind].astype(F32)

    def first(self):
        for way in (1, -1):
            if self.reach[way] > 3:
                self.post(way, 3, self.own(4 * way), 2)
        for way in (1, -1):
            if self.reach[way] > 2:
                self.post(way, 2, self.own(3 * way), 1)
        for way in (1, -1):
            if self.reach[way] > 0:
                self.post(way, 0, self.own(way), 1)

    def second(self):
        for way in (1, -1):
            if self.reach[way] > 1:
                value = self.own(2 * way)
                for kind in (2, 3):
                    if self.reach[way] > kind:
                        value = value + self.took(way, kind)
                self.post(way, 1, value, 2)

    def total(self):
        value = self.own(0)
        for kind in (0, 1):
            for way in (1, -1):
                if self.reach[way] > kind:
                    value = value + self.took(way, kind)
        return value


def kernel(
    student_ref, teacher_feat_ref, proto_ref, teacher_ref, center_ref, new_ref, feat_ref, raw_ref,
    feats, masters, half, half_t, proto_inv, unit, rows, rows_t, row_inv,
    t_rows, s_exp, t_exp, s_sum, t_sum, scale, den_y, den_z, grads, s_part, t_part,
    s_wire, s_land, t_wire, t_land, s_chunk, s_wire_z, s_land_z, t_chunk, t_land_z, final,
    raw, wire_c, land_c, wire_x, land_x, own_x, wire_l, land_l,
    send_sem, recv_sem,
):
    d, f = lax.axis_index("dp"), lax.axis_index("fsdp")
    c, zl, x = lax.rem(d, NC), lax.rem(d // NC, NZL), d // (NC * NZL)
    y, zh = f // NZH, lax.rem(f, NZH)
    bot, count = proto_ref.shape
    s_rows = unit.shape[0]
    t_pad = t_sum.shape[0]
    width = feats.shape[3]
    tiles = count // COLS
    s_tiles, t_tiles = s_sum.shape[0] // LANES, t_pad // LANES
    share = s_rows // (NY * NZH)
    images = share // STUDENT_CROPS
    t_used = NY * NZH * 8

    def at(x_=x, zl_=zl, c_=c, y_=y, zh_=zh):
        return ((x_ * NZL + zl_) * NC + c_, y_ * NZH + zh_)

    def wrap(value, size):
        return lax.rem(value + size, size)

    def to_y(s):
        return at(y_=wrap(y + s, NY))

    def to_x(s):
        return at(x_=wrap(x + s, NX))

    def to_zh(k):
        return at(zh_=wrap(zh + k, NZH))

    def to_zl(k):
        return at(zl_=wrap(zl + k, NZL))

    used = [0]
    started = []

    def send(src, dst, to):
        i = used[0]
        used[0] += 1
        copy = pltpu.make_async_remote_copy(
            src_ref=src, dst_ref=dst, send_sem=send_sem.at[i], recv_sem=recv_sem.at[i],
            device_id=to, device_id_type=MESH,
        )
        copy.start()
        started.append(copy)
        return copy

    partners = (
        [to_y(k) for k in range(1, NY)]
        + [to_zh(k) for k in range(1, NZH)]
        + [to_zl(k) for k in range(1, NZL)]
        + [at(c_=1 - c)]
        + [to_x(k) for k in range(1, NX)]
    )
    barrier = pltpu.get_barrier_semaphore()
    for partner in partners:
        pl.semaphore_signal(barrier, inc=1, device_id=partner, device_id_type=MESH)

    teacher_feat = teacher_feat_ref[...].astype(F32)
    wide = [student_ref[...].astype(F32)]
    if width > s_rows:
        wide.append(jnp.zeros((12, width - s_rows), F32))
    slot = jnp.concatenate(
        [jnp.concatenate(wide, axis=1), jnp.zeros((4, width), F32)], axis=0
    )
    t_count = teacher_feat.shape[1]
    fill = [jnp.zeros((4, t_pad - t_count), F32)] if t_pad > t_count else []
    last = []
    for q in range(3):
        last += [teacher_feat[4 * q : 4 * q + 4]] + fill
    if width > 3 * t_pad:
        last.append(jnp.zeros((4, width - 3 * t_pad), F32))
    last = jnp.concatenate(last, axis=1)
    low = jnp.concatenate([jnp.zeros((4, width), F32), last], axis=0)
    line = lax.broadcasted_iota(jnp.int32, (16, width), 0)
    feats[y, zh] = jnp.where(
        line < 12, slot, jnp.concatenate([jnp.zeros((8, width), F32), low], axis=0)
    ).astype(BF16)
    student_own = proto_ref[pl.ds(pl.multiple_of(d * 16, 16), 16), :].astype(F32)
    own_master = MOMENTUM * teacher_ref[...] + (1.0 - MOMENTUM) * student_own
    new_ref[...] = own_master
    masters[d] = own_master
    pl.semaphore_wait(barrier, len(partners))

    def along_z(buffer):
        return [send(buffer.at[y, zh], buffer.at[y, zh], to_zh(k)) for k in range(1, NZH)]

    def along_y(buffer):
        def spot_of(k):
            return lambda dy: buffer.at[wrap(y + dy, NY), wrap(zh - k, NZH)]

        return [
            Spread(send, spot_of(k), to_y, NY, k % 2, NY if 2 * k == NZH else 2)
            for k in range(NZH)
        ]

    order = sorted(range(1, NZH), key=lambda k: (min(k, NZH - k), k))
    feat_z = along_z(feats)
    feat_y = along_y(feats)
    feat_y[0].first()

    across = []

    def to_sibling(block):
        across.append(send(block, block, at(c_=1 - c)))

    def master_of(k):
        return lambda dx: masters.at[(wrap(x + dx, NX) * NZL + wrap(zl - k, NZL)) * NC + c]

    master_z = [send(masters.at[d], masters.at[d], to_zl(k)) for k in range(1, NZL)]
    master_x = [Spread(send, master_of(k), to_x, NX, k % 2) for k in range(NZL)]
    master_x[0].first()
    to_sibling(masters.at[d])

    @pl.loop(0, tiles)
    def _(n):
        at_n = pl.ds(pl.multiple_of(n * COLS, COLS), COLS)
        block = proto_ref[:, at_n].astype(F32)
        inverse = lax.rsqrt(jnp.sum(block * block, axis=0, keepdims=True) + EPSILON)
        normed = block * inverse
        half[:, at_n] = normed.astype(BF16)
        half_t[at_n, :] = normed.T.astype(BF16)
        proto_inv[:, at_n] = inverse

    feat_y[0].second()
    for k in order:
        feat_z[k - 1].wait_recv()
        feat_y[k].first()
    for k in order:
        feat_y[k].second()
    for k in range(1, NZL):
        master_z[k - 1].wait_recv()
        master_x[k].first()
        to_sibling(master_of(k)(0))
    for copy, block in master_x[0].arrivals():
        copy.wait_recv()
        to_sibling(block)
    for one in feat_y:
        one.last()

    slots = feats[...].reshape(NY * NZH * 16, width)
    spots = lax.broadcasted_iota(jnp.int32, (bot, NY * NZH * 16), 1)
    wanted = lax.broadcasted_iota(jnp.int32, (bot, NY * NZH * 16), 0)
    owner = lax.shift_right_logical(wanted * 5462, 16)
    pick_s = (spots == owner * 16 + (wanted - owner * 12)).astype(F32).astype(BF16)
    pick_t = (spots == owner * 16 + 12 + (wanted & 3)).astype(F32).astype(BF16)
    student_t = jnp.dot(pick_s, slots[:, :s_rows], preferred_element_type=F32)
    inverse = lax.rsqrt(jnp.sum(student_t * student_t, axis=0, keepdims=True) + EPSILON)
    rows_t[...] = (student_t * inverse).astype(BF16)
    student = student_t.T
    inverse = lax.rsqrt(jnp.sum(student * student, axis=1, keepdims=True) + EPSILON)
    normed = student * inverse
    unit[...] = normed
    rows[...] = normed.astype(BF16)
    row_inv[...] = jnp.broadcast_to(inverse, row_inv.shape)
    pieces = jnp.dot(pick_t, slots[:, : 3 * t_pad], preferred_element_type=F32)
    place = lax.broadcasted_iota(jnp.int32, (bot, t_pad), 0)
    owner = lax.shift_right_logical(place * 5462, 16)
    quarter = lax.shift_right_logical(place - owner * 12, 2)
    teacher_t = jnp.where(
        quarter == 0,
        pieces[:, :t_pad],
        jnp.where(quarter == 1, pieces[:, t_pad : 2 * t_pad], pieces[:, 2 * t_pad :]),
    )
    teacher = teacher_t.T
    inverse = lax.rsqrt(jnp.sum(teacher * teacher, axis=1, keepdims=True) + EPSILON)
    to_row = lax.broadcasted_iota(jnp.int32, (t_pad, t_pad), 0)
    from_row = lax.broadcasted_iota(jnp.int32, (t_pad, t_pad), 1)
    place = to_row & 7
    moved = (from_row == lax.shift_right_logical(to_row, 3) * (2 * images) + place) & (place < 2 * images)
    t_rows[...] = jnp.dot(
        moved.astype(F32).astype(BF16), (teacher * inverse).astype(BF16), preferred_element_type=F32
    ).astype(BF16)

    def fold(values):
        return sum(values[:, i : i + LANES] for i in range(0, values.shape[1], LANES))

    s_sum[...] = jnp.zeros_like(s_sum)
    t_sum[...] = jnp.zeros_like(t_sum)
    s_part[...] = jnp.zeros_like(s_part)
    t_part[...] = jnp.zeros_like(t_part)

    def student_tile(n):
        at_n = pl.ds(pl.multiple_of(n * WIDE, WIDE), WIDE)
        logits = jnp.dot(rows[...], half[:, at_n], preferred_element_type=F32)
        value = jnp.exp(logits * (1.0 / STUDENT_TEMP))
        s_exp[:, at_n] = value
        s_sum[:s_rows, :] += fold(value)
        s_part[...] += jnp.dot(value.astype(BF16), half_t[at_n, :], preferred_element_type=F32)

    def masters_on(k):
        for copy, block in master_x[k].arrivals():
            copy.wait_recv()
            to_sibling(block)

    early = count // WIDE * 3 // 4
    pl.loop(0, early)(student_tile)
    if NZL > 1:
        masters_on(1)
    pl.loop(early, count // WIDE)(student_tile)

    part = s_part[...]
    s_part[...] = part - unit[...] * jnp.sum(unit[...] * part, axis=1, keepdims=True)

    y_rows = s_rows // NY
    piece = y_rows // 2

    def own_s(h):
        def own(dy):
            start = wrap(y + dy, NY) * y_rows + h * piece
            return s_part[pl.ds(pl.multiple_of(start, 8), piece), :]

        return own

    s_ring = [
        Gathered(send, own_s(h), s_wire.at[h], s_land.at[h], to_y, NY, h) for h in range(2)
    ]
    for one in s_ring:
        one.first()
    for k in range(2, NZL):
        masters_on(k)
    for copy in across:
        copy.wait_recv()

    @pl.loop(0, count // WIDE)
    def _(n):
        at_n = pl.ds(pl.multiple_of(n * WIDE, WIDE), WIDE)
        block = masters[:, :, at_n].reshape(bot, WIDE)
        inverse = lax.rsqrt(jnp.sum(block * block, axis=0, keepdims=True) + EPSILON)
        logits = jnp.dot(t_rows[...], (block * inverse).astype(BF16), preferred_element_type=F32)
        value = jnp.exp((logits - center_ref[:, at_n]) * (1.0 / TEACHER_TEMP))
        t_exp[:, at_n] = value
        t_sum[...] += fold(value)
        t_part[...] += jnp.dot(value.astype(BF16), half_t[at_n, :], preferred_element_type=F32)

    def own_t(dy):
        return t_part[pl.ds(pl.multiple_of(wrap(y + dy, NY) * (8 * NZH), 8), 8 * NZH), :]

    line = lax.broadcasted_iota(jnp.int32, (8, LANES), 0)
    packed = jnp.zeros((8, LANES), F32)
    for i in range(s_tiles + t_tiles):
        block = (
            s_sum[i * LANES : (i + 1) * LANES, :]
            if i < s_tiles
            else t_sum[(i - s_tiles) * LANES : (i - s_tiles + 1) * LANES, :]
        )
        packed = jnp.where(line == i, jnp.sum(block.T, axis=0, keepdims=True), packed)
    den_y[0] = packed
    dens = [send(den_y.at[0], den_y.at[k], to_y(k)) for k in range(1, NY)]
    t_ring = Gathered(send, own_t, t_wire, t_land, to_y, NY, 1)
    t_ring.first()
    for one in s_ring:
        one.second()
    t_ring.second()
    for copy in dens:
        copy.wait_recv()
    den_z[0] = jnp.sum(den_y[...], axis=0)
    dens = [send(den_z.at[0], den_z.at[k], to_zh(k)) for k in range(1, NZH)]
    s_chunk[...] = jnp.concatenate([one.total() for one in s_ring], axis=0).reshape(s_chunk.shape)
    s_met = []
    for k in range(1, NZH):
        s_wire_z[k] = s_chunk[wrap(zh + k, NZH)].astype(BF16)
        s_met.append(send(s_wire_z.at[k], s_land_z.at[k], to_zh(k)))
    t_chunk[...] = t_ring.total().reshape(t_chunk.shape)
    t_met = [
        send(t_chunk.at[wrap(zh + k, NZH)], t_land_z.at[k], to_zh(k)) for k in range(1, NZH)
    ]
    for copy in dens:
        copy.wait_recv()
    total = jnp.sum(den_z[...], axis=0)
    inverse = (PROTO / 16.0 / STUDENT_TEMP) / jnp.where(total > 0.0, total, 1.0)
    crop = lax.broadcasted_iota(jnp.int32, (LANES, LANES), 0) & (STUDENT_CROPS - 1)
    copies = jnp.where(crop < GLOBAL_CROPS, F32(GLOBAL_CROPS - 1), F32(GLOBAL_CROPS))
    for i in range(s_tiles + t_tiles):
        block = jnp.broadcast_to(inverse[i : i + 1, :], (LANES, LANES)).T
        scale[i * LANES : (i + 1) * LANES, :] = block * copies if i < s_tiles else block

    def partner_of(prob, i, position):
        first, second = prob[2 * i : 2 * i + 1], prob[2 * i + 1 : 2 * i + 2]
        return jnp.where(position == 0, second, jnp.where(position == 1, first, first + second))

    position = lax.broadcasted_iota(jnp.int32, (STUDENT_CROPS, count), 0)

    @pl.loop(0, NY * NZH // 2)
    def _(i):
        out = []
        for e in range(2):
            g = i * 2 + e
            at_t = pl.ds(pl.multiple_of(g * 8, 8), 8)
            at_s = pl.ds(pl.multiple_of(g * share, 8), share)
            t_scale = scale[pl.ds(pl.multiple_of(s_tiles * LANES + g * 8, 8), 8), :1]
            prob = t_exp[at_t, :] * t_scale
            value = s_exp[at_s, :] * scale[at_s, :1]
            for a in range(images):
                out.append(value[8 * a : 8 * a + 8] - partner_of(prob, a, position))
        both = pl.ds(pl.multiple_of(i * 2 * share, 16), 2 * share)
        grads[both, :] = jnp.concatenate(out, axis=0).astype(BF16)

    wide = count // 2

    def proto_tile(q):
        def tile(n):
            at_n = pl.ds(pl.multiple_of(n * WIDE, WIDE), WIDE)
            at_q = pl.ds(pl.multiple_of(n * WIDE - q * wide, WIDE), WIDE)
            part = jnp.dot(rows_t[...], grads[:, at_n], preferred_element_type=F32)
            inverse = proto_inv[:, at_n]
            normed = proto_ref[:, at_n].astype(F32) * inverse
            along = jnp.sum(normed * part, axis=0, keepdims=True)
            part = inverse * (part - normed * along)
            raw[q, :, :, :, at_q] = part.reshape(NX * NZL, NC, 16, WIDE)
            wire_c[q, :, :, at_q] = (
                raw[q, :, pl.ds(1 - c, 1), :, at_q].reshape(NX * NZL, 16, WIDE).astype(BF16)
            )

        return tile

    def own_raw(q, k):
        def own(dx):
            slot = wrap(x + dx, NX) * NZL + k
            return raw[q, slot, c] + land_c[q, slot].astype(F32)

        return own

    over = []
    raw_x = []
    for q in range(2):
        pl.loop(q * wide // WIDE, (q + 1) * wide // WIDE)(proto_tile(q))
        over.append(send(wire_c.at[q], land_c.at[q], at(c_=1 - c)))
        raw_x.append(
            [
                Gathered(
                    send, own_raw(q, k), wire_x.at[q, k], land_x.at[q, k], to_x, NX, (k + q) % 2
                )
                for k in range(NZL)
            ]
        )

    def on_x(q):
        over[q].wait_recv()
        for one in raw_x[q]:
            one.first()
            one.second()

    on_x(0)

    s_value, t_value = s_chunk[zh], t_chunk[zh]
    for k in range(1, NZH):
        s_met[k - 1].wait_recv()
        t_met[k - 1].wait_recv()
        s_value = s_value + s_land_z[k].astype(F32)
        t_value = t_value + t_land_z[k]
    at_s = pl.ds(pl.multiple_of(f * share, 8), share)
    s_value = s_value * scale[at_s, :1]
    t_value = t_value * scale[pl.ds(pl.multiple_of(s_tiles * LANES + f * 8, 8), 8), :1]
    position = lax.broadcasted_iota(jnp.int32, (STUDENT_CROPS, bot), 0)
    value = s_value - jnp.concatenate(
        [partner_of(t_value, a, position) for a in range(images)], axis=0
    )
    normed = unit[at_s, :]
    value = value - normed * jnp.sum(normed * value, axis=1, keepdims=True)
    final[y, zh] = (value * row_inv[at_s, :1]).astype(BF16)
    final_z = along_z(final)
    final_y = along_y(final)
    final_y[0].first()

    on_x(1)
    final_y[0].second()
    for k in order:
        final_z[k - 1].wait_recv()
        final_y[k].first()
    raw_met = []
    for q in range(2):
        for k in range(NZL):
            own_x[q, k] = raw_x[q][k].total()
        for k in range(1, NZL):
            wire_l[q, k] = own_x[q, wrap(zl + k, NZL)].astype(BF16)
            raw_met.append(send(wire_l.at[q, k], land_l.at[q, k], to_zl(k)))
        if q == 0:
            for k in order:
                final_y[k].second()
    for q in range(2):
        value = own_x[q, zl]
        for k in range(1, NZL):
            raw_met[q * (NZL - 1) + k - 1].wait_recv()
            value = value + land_l[q, k].astype(F32)
        raw_ref[:, q * wide : (q + 1) * wide] = value
    for one in final_y:
        one.last()
    for i in range(NY):
        feat_ref[i * y_rows : (i + 1) * y_rows, :] = final[i].astype(F32).reshape(y_rows, bot)

    for copy in started:
        copy.wait_send()


def call(student, teacher_feat, proto, teacher, center):
    bot, count = proto.shape
    s_rows, t_rows = student.shape[1], teacher_feat.shape[1]
    y_rows = s_rows // NY
    z_rows = y_rows // NZH
    vmem = pltpu.VMEM
    s_pad, t_pad = up(s_rows, LANES), up(t_rows, LANES)
    width = max(s_rows, 3 * t_pad)
    copies = (
        (NZH - 1) + NZH * (NY - 1)
        + (NZL - 1) + NZL * (NX - 1) + NZL * NX
        + (NY - 1) + (NZH - 1)
        + 3 * (NY - 1) + 2 * (NZH - 1) + (NZH - 1) + NZH * (NY - 1)
        + 2 + 2 * NZL * (NX - 1) + 2 * (NZL - 1)
    )
    return pl.pallas_call(
        kernel,
        out_shape=(
            pltpu.VMEM((16, count), F32),
            pltpu.VMEM((s_rows, bot), F32),
            pltpu.VMEM((16, count), F32),
        ),
        in_specs=[pl.BlockSpec(memory_space=pltpu.VMEM)] * 5,
        out_specs=[pl.BlockSpec(memory_space=pltpu.VMEM)] * 3,
        scratch_shapes=[
            vmem((NY, NZH, 16, width), BF16),
            vmem((NX * NZL * NC, 16, count), F32),
            vmem((bot, count), BF16),
            vmem((count, bot), BF16),
            vmem((1, count), F32),
            vmem((s_rows, bot), F32),
            vmem((s_rows, bot), BF16),
            vmem((bot, s_rows), BF16),
            vmem((s_rows, LANES), F32),
            vmem((t_pad, bot), BF16),
            vmem((s_rows, count), F32),
            vmem((t_pad, count), F32),
            vmem((s_pad, LANES), F32),
            vmem((t_pad, LANES), F32),
            vmem((s_pad + t_pad, LANES), F32),
            vmem((NY, 8, LANES), F32),
            vmem((NZH, 8, LANES), F32),
            vmem((s_rows, count), BF16),
            vmem((s_rows, bot), F32),
            vmem((t_pad, bot), F32),
            vmem((2, 2, 4, y_rows // 2, bot), BF16),
            vmem((2, 2, 4, y_rows // 2, bot), BF16),
            vmem((2, 4, 8 * NZH, bot), F32),
            vmem((2, 4, 8 * NZH, bot), F32),
            vmem((NZH, z_rows, bot), F32),
            vmem((NZH, z_rows, bot), BF16),
            vmem((NZH, z_rows, bot), BF16),
            vmem((NZH, 8, bot), F32),
            vmem((NZH, 8, bot), F32),
            vmem((NY, NZH, z_rows, bot), BF16),
            vmem((2, NX * NZL, NC, 16, count // 2), F32),
            vmem((2, NX * NZL, 16, count // 2), BF16),
            vmem((2, NX * NZL, 16, count // 2), BF16),
            vmem((2, NZL, 2, 2, 16, count // 2), BF16),
            vmem((2, NZL, 2, 2, 16, count // 2), BF16),
            vmem((2, NZL, 16, count // 2), F32),
            vmem((2, NZL, 16, count // 2), BF16),
            vmem((2, NZL, 16, count // 2), BF16),
            pltpu.SemaphoreType.DMA((copies,)),
            pltpu.SemaphoreType.DMA((copies,)),
        ],
        compiler_params=pltpu.CompilerParams(
            collective_id=0, has_side_effects=True, vmem_limit_bytes=56 * 1024 * 1024
        ),
    )(student, teacher_feat, proto, teacher, center)


def body(student_feat, teacher_feat, student_proto, teacher_proto, center):
    return tuple(
        call(student_feat.T, teacher_feat.T, student_proto, teacher_proto, center.reshape(1, -1))
    )


def solution(mesh):
    placed = (P("dp", "fsdp"), P("dp", "fsdp"), P(None, "fsdp"), P("dp", "fsdp"), P("fsdp"))
    return jax.shard_map(
        body,
        mesh=mesh,
        in_specs=placed,
        out_specs=(P("dp", "fsdp"), P("dp", None), P("dp", "fsdp")),
        check_vma=False,
    )
```
